32 devices in a mesh: dp: 4 (over z), expert: 4 (over y, x), seq: 2 (over core).
Axes of the slice: x: 2, y: 2, z: 4, core: 2. Of those that a mesh axis runs over, the one named last changes fastest.
Arguments:
- queries: bfloat16 [4096, 2560], P(('dp', 'expert', 'seq')), may hold values from -64 to 64
- memory: bfloat16 [2, 512, 2560], P(None, ('dp', 'expert', 'seq')), may hold values from -6 to 6
- residual: bfloat16 [4096, 2560], P(('dp', 'expert', 'seq')), may hold values from -3 to 3
- norm_gain: float32 [2560], replicated, may hold values from 0.5 to 1.5
- expert_ids: int32 [4096, 2], P(('dp', 'expert', 'seq')), may hold values from 0 to 3, all different within a row; in each aligned block of 128 rows (0 to 127, 128 to 255, ...) at most 80 rows name the same one
- route_gates: float32 [4096, 2], P(('dp', 'expert', 'seq')), may hold values from 0.1 to 1
- weight_in: bfloat16 [4, 2560, 320], P('expert'), may hold values from -0.125 to 0.125
- weight_out: bfloat16 [4, 320, 2560], P('expert'), may hold values from -0.3125 to 0.3125
- layer_grad: bfloat16 [4096, 2560], P(('dp', 'expert', 'seq')), may hold values from -6 to 6
Outputs:
- layer_output: bfloat16 [4096, 2560], P(('dp', 'expert', 'seq'))
- weight_grads: float32 [4, 2560, 320], P('expert', ('dp', 'seq'))
The draws below stay inside these ranges and needn't reach their ends.
Inputs may be any that keep to these rules, and one draw needn't show every extreme that they name: `expert_ids`: within each aligned block of 128 tokens (the tokens of one device) no expert is named more than 80 times, and in some block one expert is named exactly 80 times.
All inputs are finite; a program needn't handle non-finite values.
Results may differ from the reference program's by a relative error of at most 0.01.
Values may be sent and summed in bfloat16 or wider, within the bound.
No kernel may reach another device: no remote copies, remote signals or barrier semaphores. Data moves between devices by JAX's collectives and lax.ppermute only.
A program may use at most 64 MiB of HBM per device.

```python
import math
import jax
import jax.numpy as jnp
import numpy as np
from jax import lax

D = 2560
HEADS = 40
HEAD_SIZE = 64
FF_W = 320
TOK_DEV = 128
TOK_G = 256
GROUPS = 16
TOKENS = 4096
MEM = 32
EXPERTS = 4
CAP = 80


def draw_queries(key, part):
    values = jax.random.truncated_normal(jax.random.fold_in(key, 3), -6.0, 6.0, (TOKENS, D), jnp.float32)
    return values.astype(jnp.bfloat16)


def draw_memory(key, part):
    values = jax.random.truncated_normal(jax.random.fold_in(key, 5), -6.0, 6.0, (2, GROUPS * MEM, D), jnp.float32)
    return values.astype(jnp.bfloat16)


def spiked(entries, stream_key, source, target, shards_of, factor):
    def block_of(dim):
        return (jnp.arange(entries.shape[dim]) // (entries.shape[dim] // shards_of)).reshape((-1,) + (1,) * (entries.ndim - 1 - dim))

    near = jax.random.permutation(stream_key, shards_of)[block_of(target)]
    second = (block_of(target) + shards_of // 2) % shards_of
    return jnp.where((block_of(source) == near) | (block_of(source) == second), factor * entries, entries)


def steps_of(rng, dims, split, low, high):
    def one(axis_at, parts):
        steps = jax.random.uniform(jax.random.fold_in(jax.random.fold_in(rng, 6), axis_at), (parts,), jnp.float32, low / len(split), high / len(split))
        return jnp.repeat(jnp.exp(steps), dims[axis_at] // parts).reshape((-1,) + (1,) * (len(dims) - axis_at - 1))

    gain = one(*split[0])
    for cut in split[1:]:
        gain = gain * one(*cut)
    return gain


def routed_block(own_key, own, number, rows, number_of, top, limit, slope):
    ranking = jax.random.permutation(own_key, number_of)
    packed, common = shares(number_of, rows * top, limit, slope, True), shares(number_of, rows * top, limit, slope, False)
    places = jnp.arange(number_of)

    def named(tallies, rotation):
        used = int((tallies > 0).sum())
        fixed = max(1, used // 4)
        moved = fixed + (places - fixed + rotation * (used - fixed)) % max(1, number_of - fixed)
        return jnp.zeros((number_of,), jnp.int32).at[ranking[jnp.where(places < fixed, places, moved)]].set(jnp.asarray(tallies, jnp.int32))

    tallies = jnp.where(number % 4 == 0, named(packed, number // 4), named(common, number - number // 4 - 1))
    mixed = jax.random.permutation(jax.random.fold_in(own, 3), number_of)
    giver, taker = mixed[0:number_of // 2 * 2:2], mixed[1:number_of // 2 * 2:2]
    room = jnp.minimum(tallies[giver] - 1, limit - tallies[taker]) // 2
    room = jnp.where((giver == ranking[0]) | (taker == ranking[0]) | (tallies[taker] == 0), 0, jnp.maximum(room, 0))
    moved = jax.random.randint(jax.random.fold_in(own, 4), (number_of // 2,), 0, 1 << 20) % (room + 1)
    tallies = tallies.at[giver].add(-moved).at[taker].add(moved)
    items = jnp.searchsorted(jnp.cumsum(tallies), jnp.arange(rows * top), side="right").astype(jnp.int32)
    listing = items.reshape(top, rows).T
    listing = listing[jax.random.permutation(jax.random.fold_in(own, 1), rows)]
    rotation = jax.random.randint(jax.random.fold_in(own, 2), (rows, 1), 0, top)
    return jnp.take_along_axis(listing, (jnp.arange(top)[None, :] + rotation) % top, axis=1)


def shares(amount, total, most, skew, full):
    weights = [(1 << 20) // math.isqrt(rank ** skew) + 1 for rank in range(1, amount + 1)]
    largest = most if full else min(most, max(-(-total // amount), total * weights[0] // sum(weights)))
    least = 1 if total - largest >= amount - 1 else 0
    counts, spare = [largest] + [least] * (amount - 1), total - largest - least * (amount - 1)
    while spare > 0:
        free = [i for i in range(1, amount) if counts[i] < largest] or [i for i in range(1, amount) if counts[i] < most]
        pool, budget = sum([weights[i] for i in free]), spare
        for i in free:
            extra = min(most - counts[i], max(1, budget * weights[i] // pool), spare)
            counts[i] = counts[i] + extra
            spare = spare - extra
    return np.array(counts)


def centred(stream_key, extent, deviation, reach, shards=(), kind=jnp.bfloat16):
    values = jax.random.normal(stream_key, extent, jnp.float32) * deviation
    if len(shards) > 0:
        values = steps_of(stream_key, extent, shards, -0.22, 0.18) * values
    return jnp.clip(values, min=-reach, max=reach).astype(kind)


def gaussian_with(stream_key, dims, spread, limit, pieces, heavy, kind=jnp.bfloat16):
    result = spread * jax.random.normal(stream_key, dims, jnp.float32)
    if pieces:
        result = result * steps_of(stream_key, dims, pieces, -0.22, 0.18)
    return jnp.clip(spiked(result, jax.random.fold_in(stream_key, 3), *heavy), -limit, limit).astype(kind)


def setup_inputs(seed: int = 0) -> dict:
    streams_of = jax.random.split(jax.random.key(seed), 10)
    queries = draw_queries(jax.random.fold_in(streams_of[9], 71), 0)
    memory = draw_memory(jax.random.fold_in(streams_of[9], 71), 0)
    residual = centred(streams_of[2], (TOKENS, D), 0.5, 3.0, ((0, 32),))
    norm_gain = jnp.clip(1.0 + 0.1 * jax.random.normal(streams_of[3], (D,), jnp.float32), 0.5, 1.5)
    expert_ids_keys = jax.random.split(jax.random.fold_in(streams_of[4], 1), TOKENS // TOK_DEV)
    expert_ids_turns = jax.random.permutation(jax.random.fold_in(streams_of[4], 3), TOKENS // TOK_DEV)
    expert_ids = jax.vmap(lambda own, number: routed_block(jax.random.fold_in(streams_of[4], 2), own, number, TOK_DEV, EXPERTS, 2, CAP, 2))(expert_ids_keys, expert_ids_turns).reshape((TOKENS, 2))
    route_gates = jnp.clip(jnp.exp(math.log(1.0) - 2.3025851 * jax.random.uniform(streams_of[5], (TOKENS, 2), jnp.float32) ** steps_of(streams_of[5], (TOKENS, 2), ((0, 32),), -0.2, 0.2)), 0.1, 1.0)
    weight_in = centred(streams_of[6], (EXPERTS, D, FF_W), D ** -0.5, 0.125, ((0, 4),))
    weight_out = centred(streams_of[7], (EXPERTS, FF_W, D), FF_W ** -0.5, 0.3125, ((0, 4),))
    layer_grad = gaussian_with(streams_of[8], (TOKENS, D), 1.0, 6.0, ((0, 32),), (0, 1, 32, 2.75))
    return dict(queries=queries, memory=memory, residual=residual, norm_gain=norm_gain, expert_ids=expert_ids, route_gates=route_gates, weight_in=weight_in, weight_out=weight_out, layer_grad=layer_grad)


def gelu_tanh(values):
    return jax.nn.gelu(values, approximate=True)

def attend_group(inputs):
    group_queries, group_keys, group_values = inputs
    query_per_head = group_queries.astype(jnp.float32).reshape(TOK_G, HEADS, HEAD_SIZE)
    key_per_head = group_keys.astype(jnp.float32).reshape(MEM, HEADS, HEAD_SIZE)
    value_per_head = group_values.astype(jnp.float32).reshape(MEM, HEADS, HEAD_SIZE)
    attention_scores = jnp.einsum('gvc,rvc->vgr', query_per_head, key_per_head) * HEAD_SIZE ** (-0.5)
    attention_probabilities = jax.nn.softmax(attention_scores, axis=-1).astype(jnp.bfloat16)
    attended_values = jnp.einsum('nqz,zny->qny', attention_probabilities.astype(jnp.float32), value_per_head)
    return attended_values.astype(jnp.bfloat16).reshape(TOK_G, D)

def expert_work(inputs):
    token_rows, grad_rows, matrix_in, matrix_out = inputs
    preact = jnp.dot(token_rows, matrix_in, preferred_element_type=jnp.float32)
    activated, gelu_back = jax.vjp(gelu_tanh, preact)
    hidden = activated.astype(jnp.bfloat16)
    expert_outputs = jnp.dot(hidden, matrix_out, preferred_element_type=jnp.float32).astype(jnp.bfloat16)
    hidden_grad = jnp.dot(grad_rows, matrix_out.T, preferred_element_type=jnp.float32)
    preact_grad = gelu_back(hidden_grad)[0].astype(jnp.bfloat16)
    grad_in = jnp.dot(token_rows.T, preact_grad, preferred_element_type=jnp.float32)
    return (expert_outputs, grad_in)

def reference(queries, memory, residual, norm_gain, expert_ids, route_gates, weight_in, weight_out, layer_grad):
    token_count = queries.shape[0]
    group_count = token_count // TOK_G
    attended_values = lax.map(attend_group, (queries.reshape(group_count, TOK_G, D), memory[0].reshape(group_count, MEM, D), memory[1].reshape(group_count, MEM, D)))
    attended_values = attended_values.reshape(token_count, D)
    stream = residual.astype(jnp.float32) + attended_values.astype(jnp.float32)
    scale_factor = lax.rsqrt(lax.optimization_barrier(jnp.mean(stream * stream, axis=-1, keepdims=True)) + 1e-06)
    normed = (stream * scale_factor * norm_gain).astype(jnp.bfloat16)
    block_count = token_count // TOK_DEV
    pair_ids = expert_ids.reshape(block_count, 2 * TOK_DEV).astype(jnp.int32)
    one_hot = (pair_ids[:, :, None] == jnp.arange(EXPERTS, dtype=jnp.int32)[None, None, :]).astype(jnp.int32)
    earlier = (jnp.cumsum(one_hot, axis=1) - one_hot).astype(jnp.int32)
    slot_index = lax.optimization_barrier(jnp.sum(earlier * one_hot, axis=2)).astype(jnp.int32)
    buffer_rows = (jnp.arange(block_count, dtype=jnp.int32)[:, None] * CAP + slot_index).reshape(-1).astype(jnp.int32)
    flat_ids = pair_ids.reshape(-1)
    pair_rows = jnp.repeat(normed, 2, axis=0)
    pair_grads = (route_gates[:, :, None] * layer_grad.astype(jnp.float32)[:, None, :]).astype(jnp.bfloat16).reshape(-1, D)
    empty_buffer = jnp.zeros((EXPERTS, block_count * CAP, D), jnp.bfloat16)
    buffer_tokens = empty_buffer.at[flat_ids, buffer_rows].set(pair_rows)
    buffer_grads = empty_buffer.at[flat_ids, buffer_rows].set(pair_grads)
    expert_outputs, weight_grads = lax.map(expert_work, (buffer_tokens, buffer_grads, weight_in, weight_out))
    picked = expert_outputs[flat_ids, buffer_rows].reshape(token_count, 2, D)
    expert_mix = lax.optimization_barrier(jnp.sum(picked.astype(jnp.float32) * route_gates[:, :, None], axis=1))
    return ((stream + expert_mix).astype(jnp.bfloat16), weight_grads)
```

```python
import functools

import jax
import jax.numpy as jnp
from jax import lax
from jax.experimental import pallas as pl
from jax.experimental.pallas import tpu as pltpu
from jax.sharding import PartitionSpec as P

HEAD_SIZE = 64
GROUP = 256
CHUNK = 512
VMEM_LIMIT = 24 * 1024 * 1024
GELU_C = 0.7978845608028654
GELU_A = 0.044715
BF16 = jnp.bfloat16
F32 = jnp.float32


def params():
    return pltpu.CompilerParams(vmem_limit_bytes=VMEM_LIMIT)


def call(kernel, out_shapes, scratch=()):
    return pl.pallas_call(
        kernel, out_shape=out_shapes, scratch_shapes=list(scratch), compiler_params=params()
    )


def shape(dims, dtype):
    return jax.ShapeDtypeStruct(dims, dtype)


def slots_of(ids_ref):
    tokens = ids_ref.shape[1]
    me = lax.axis_index("expert")
    expert = lax.broadcasted_iota(jnp.int32, (8, tokens), 0) ^ me
    first = ids_ref[0:1, :] == expert
    chosen = first | (ids_ref[1:2, :] == expert)
    earlier = lax.broadcasted_iota(jnp.int32, (tokens, tokens), 0) < lax.broadcasted_iota(
        jnp.int32, (tokens, tokens), 1
    )
    count = jnp.dot(
        jnp.where(chosen, 1.0, 0.0).astype(BF16),
        jnp.where(earlier, 1.0, 0.0).astype(BF16),
        preferred_element_type=F32,
    )
    return jnp.where(chosen, count.astype(jnp.int32), -1), first


def gates_of(gates_ref, first):
    return jnp.where(first, gates_ref[0:1, :], gates_ref[1:2, :])


def one_hot(slots, k, capacity):
    tokens = slots.shape[1]
    return lax.broadcasted_iota(jnp.int32, (capacity, tokens), 0) == slots[k : k + 1, :]


def as_bf16(mask):
    return jnp.where(mask, 1.0, 0.0).astype(BF16)


def dispatch_grads(count, ids_ref, gates_ref, grad_ref, *out_refs):
    slots, first = slots_of(ids_ref)
    gates = gates_of(gates_ref, first)
    width = grad_ref.shape[1]
    for k in range(count):
        mask = one_hot(slots, k, out_refs[k].shape[0])
        gate = jnp.sum(jnp.where(mask, gates[k : k + 1, :], 0.0), axis=1, keepdims=True)
        pick = as_bf16(mask)
        for at in range(0, width, CHUNK):
            cols = slice(at, at + CHUNK)
            rows = jnp.dot(pick, grad_ref[:, cols], preferred_element_type=F32)
            out_refs[k][:, cols] = (rows * gate).astype(BF16)


def attend(count, parts, *refs):
    ids_ref, query_ref = refs[0:2]
    memory_refs = refs[2 : 2 + parts]
    residual_ref, gain_ref = refs[2 + parts : 4 + parts]
    stream_ref = refs[4 + parts]
    out_refs = refs[5 + parts : 5 + parts + count]
    normed_ref = refs[5 + parts + count]
    tokens, width = query_ref.shape
    heads = GROUP // HEAD_SIZE
    rows = sum(ref.shape[1] for ref in memory_refs)
    own = (
        lax.broadcasted_iota(jnp.int32, (heads * rows, GROUP), 0) // rows
        == lax.broadcasted_iota(jnp.int32, (heads * rows, GROUP), 1) // HEAD_SIZE
    )
    total = jnp.zeros((tokens, 1), F32)

    def spread(which, cols):
        piece = jnp.concatenate([ref[which, :, cols] for ref in memory_refs], axis=0)
        return jnp.where(own, jnp.concatenate([piece] * heads, axis=0), jnp.zeros((), BF16))

    for at in range(0, width, GROUP):
        cols = slice(at, at + GROUP)
        scores = lax.dot_general(
            spread(0, cols), query_ref[:, cols], (((1,), (1,)), ((), ())), preferred_element_type=F32
        ) * HEAD_SIZE ** (-0.5)
        scores = scores.reshape(heads, rows, tokens)
        exponent = jnp.exp(scores - jnp.max(scores, axis=1, keepdims=True))
        probs = exponent / jnp.sum(exponent, axis=1, keepdims=True)
        attended = lax.dot_general(
            probs.reshape(heads * rows, tokens).astype(BF16),
            spread(1, cols),
            (((0,), (0,)), ((), ())),
            preferred_element_type=F32,
        ).astype(BF16)
        stream = residual_ref[:, cols].astype(F32) + attended.astype(F32)
        stream_ref[:, cols] = stream
        total = total + jnp.sum(stream * stream, axis=1, keepdims=True)
    scale = lax.rsqrt(total / width + 1e-06)
    for at in range(0, width, CHUNK):
        cols = slice(at, at + CHUNK)
        normed_ref[:, cols] = (stream_ref[:, cols] * scale * gain_ref[:, cols]).astype(BF16)
    slots, _ = slots_of(ids_ref)
    for k in range(count):
        pick = as_bf16(one_hot(slots, k, out_refs[k].shape[0]))
        for at in range(0, width, CHUNK):
            cols = slice(at, at + CHUNK)
            out_refs[k][:, cols] = jnp.dot(
                pick, normed_ref[:, cols], preferred_element_type=F32
            ).astype(BF16)


def expert_forward(count, *refs):
    rows_refs = refs[0:count]
    in_ref, out_ref = refs[count : count + 2]
    slope_refs = refs[count + 2 : 2 * count + 2]
    result_refs = refs[2 * count + 2 :]
    width = in_ref.shape[1]
    for k in range(count):
        value = lax.dot_general(
            rows_refs[k][...], in_ref[...], (((1,), (1,)), ((), ())), preferred_element_type=F32
        )
        square = value * value
        curve = jnp.tanh(GELU_C * (value + GELU_A * square * value))
        hidden = (0.5 * value * (1.0 + curve)).astype(BF16)
        slope_refs[k][...] = 0.5 * (1.0 + curve) + 0.5 * value * (1.0 - curve * curve) * (
            GELU_C * (1.0 + 3.0 * GELU_A * square)
        )
        for at in range(0, width, CHUNK):
            cols = slice(at, at + CHUNK)
            result_refs[k][:, cols] = jnp.dot(
                hidden, out_ref[:, cols], preferred_element_type=F32
            ).astype(BF16)


def preact_grads(count, grad_refs, slope_refs, out_ref):
    parts = []
    for k in range(count):
        back = lax.dot_general(
            grad_refs[k][...], out_ref[...], (((1,), (1,)), ((), ())), preferred_element_type=F32
        )
        parts.append((back * slope_refs[k][...]).astype(BF16))
    return jnp.concatenate(parts, axis=0)


def pack(block):
    rows, columns = block.shape
    full = columns // 128 * 128
    pieces = [block[:, at : at + 128] for at in range(0, full, 128)]
    pieces.append(
        jnp.concatenate([block[: rows // 2, full:], block[rows // 2 :, full:]], axis=1)
    )
    return jnp.concatenate(pieces, axis=0)


def unpack(packed, rows, columns):
    full = columns // 128 * 128
    last = packed[full // 128 * rows :, :]
    half = columns - full
    pieces = [packed[at * rows : (at + 1) * rows, :] for at in range(full // 128)]
    pieces.append(jnp.concatenate([last[:, :half], last[:, half:]], axis=0))
    return jnp.concatenate(pieces, axis=1)


def weight_grads_packed(count, shards, *refs):
    rows_refs, grad_refs = refs[0:count], refs[count : 2 * count]
    slope_refs = refs[2 * count : 3 * count]
    out_ref = refs[3 * count]
    keep_ref, send_ref = refs[3 * count + 1 :]
    back = preact_grads(count, grad_refs, slope_refs, out_ref)
    rows = jnp.concatenate([ref[...] for ref in rows_refs], axis=0)
    full = lax.dot_general(rows, back, (((0,), (0,)), ((), ())), preferred_element_type=F32)
    block = full.shape[0] // (2 * shards)
    core = lax.axis_index("seq")
    for shard in range(shards):
        even = pack(full[2 * shard * block : (2 * shard + 1) * block])
        odd = pack(full[(2 * shard + 1) * block : (2 * shard + 2) * block])
        keep_ref[shard] = jnp.where(core == 0, even, odd)
        send_ref[shard] = jnp.where(core == 0, odd, even).astype(BF16)


def weight_grads_whole(count, *refs):
    rows_refs, grad_refs = refs[0:count], refs[count : 2 * count]
    slope_refs = refs[2 * count : 3 * count]
    out_ref, result_ref = refs[3 * count :]
    back = preact_grads(count, grad_refs, slope_refs, out_ref)
    rows = jnp.concatenate([ref[...] for ref in rows_refs], axis=0)
    result_ref[...] = lax.dot_general(
        rows, back, (((0,), (0,)), ((), ())), preferred_element_type=F32
    )


def add_cores(shards, keep_ref, other_ref, own_ref, *send_refs):
    me = lax.axis_index("dp")
    own_ref[...] = keep_ref[me] + other_ref[me].astype(F32)
    for k in range(1, shards):
        send_refs[k - 1][...] = (keep_ref[me ^ k] + other_ref[me ^ k].astype(F32)).astype(BF16)


def add_replicas(own_ref, *refs):
    total = own_ref[...]
    for ref in refs[:-1]:
        total = total + ref[...].astype(F32)
    _, rows, columns = refs[-1].shape
    refs[-1][0] = unpack(total, rows, columns)


def combine(count, ids_ref, gates_ref, stream_ref, *refs):
    back_refs, out_ref = refs[0:count], refs[count]
    slots, first = slots_of(ids_ref)
    gates = gates_of(gates_ref, first).T
    width = stream_ref.shape[1]
    picks = [as_bf16(one_hot(slots, k, back_refs[k].shape[0])) for k in range(count)]
    for at in range(0, width, CHUNK):
        cols = slice(at, at + CHUNK)
        total = stream_ref[:, cols]
        for k in range(count):
            row = lax.dot_general(
                picks[k], back_refs[k][:, cols], (((0,), (0,)), ((), ())), preferred_element_type=F32
            )
            total = total + row * gates[:, k : k + 1]
        out_ref[:, cols] = total.astype(BF16)


def swap(value, axis, k):
    return lax.ppermute(value, axis, [(i, i ^ k) for i in range(lax.axis_size(axis))])


def per_device(
    queries, memory, residual, norm_gain, expert_ids, route_gates, weight_in, weight_out, layer_grad
):
    tokens, width = queries.shape
    hidden_width = weight_in.shape[2]
    experts, replicas, cores = (lax.axis_size(axis) for axis in ("expert", "dp", "seq"))
    capacity = (5 * tokens + 2 * experts - 1) // (2 * experts)
    capacity = (capacity + 15) // 16 * 16
    ids, gates = expert_ids.T, route_gates.T
    matrix_in, matrix_out = weight_in[0].T, weight_out[0]
    rows_shape = [shape((capacity, width), BF16)] * experts

    if cores == 2:
        memories = [memory, swap(memory, "seq", 1)]
    else:
        memories = [lax.all_gather(memory, "seq", axis=1, tiled=True)]
    grads = call(functools.partial(dispatch_grads, experts), rows_shape)(ids, gates, layer_grad)
    grads = [grads[0]] + [swap(grads[k], "expert", k) for k in range(1, experts)]
    stream, *rows = call(
        functools.partial(attend, experts, len(memories)),
        [shape((tokens, width), F32)] + rows_shape,
        [pltpu.VMEM((tokens, width), BF16)],
    )(ids, queries, *memories, residual, norm_gain[None])
    rows = [rows[0]] + [swap(rows[k], "expert", k) for k in range(1, experts)]
    outs = call(
        functools.partial(expert_forward, experts),
        [shape((capacity, hidden_width), F32)] * experts + rows_shape,
    )(*rows, matrix_in, matrix_out)
    slopes, results = outs[:experts], outs[experts:]
    results = [results[0]] + [swap(results[k], "expert", k) for k in range(1, experts)]

    block = width // (replicas * cores)
    if cores == 2 and replicas in (2, 4) and block % 32 == 0 and hidden_width % 128 == 64:
        packed = (replicas, block * hidden_width // 128, 128)
        keep, send = call(
            functools.partial(weight_grads_packed, experts, replicas),
            [shape(packed, F32), shape(packed, BF16)],
        )(*rows, *grads, *slopes, matrix_out)
        own, *sends = call(
            functools.partial(add_cores, replicas),
            [shape(packed[1:], F32)] + [shape(packed[1:], BF16)] * (replicas - 1),
        )(keep, swap(send, "seq", 1))
        received = [swap(sends[k - 1], "dp", k) for k in range(1, replicas)]
        grads_here = call(add_replicas, shape((1, block, hidden_width), F32))(own, *received)
    else:
        whole = call(
            functools.partial(weight_grads_whole, experts), shape((width, hidden_width), F32)
        )(*rows, *grads, *slopes, matrix_out)
        grads_here = lax.psum_scatter(whole, ("dp", "seq"), scatter_dimension=0, tiled=True)[None]

    layer_output = call(functools.partial(combine, experts), shape((tokens, width), BF16))(
        ids, gates, stream, *results
    )
    return layer_output, grads_here


def solution(mesh):
    rows = P(("dp", "expert", "seq"), None)
    return jax.shard_map(
        per_device,
        mesh=mesh,
        in_specs=(
            rows,
            P(None, ("dp", "expert", "seq"), None),
            rows,
            P(),
            rows,
            rows,
            P("expert", None, None),
            P("expert", None, None),
            rows,
        ),
        out_specs=(rows, P("expert", ("dp", "seq"), None)),
        check_vma=False,
    )
```

```python
import functools

import jax
import jax.numpy as jnp
from jax import lax
from jax.experimental import pallas as pl
from jax.experimental.pallas import tpu as pltpu
from jax.sharding import PartitionSpec as P

HEAD_SIZE = 64
GROUP = 256
CHUNK = 512
VMEM_LIMIT = 24 * 1024 * 1024
GELU_C = 0.7978845608028654
GELU_A = 0.044715
BF16 = jnp.bfloat16
F32 = jnp.float32


def params():
    return pltpu.CompilerParams(vmem_limit_bytes=VMEM_LIMIT)


def call(kernel, out_shapes, scratch=(), inputs=None):
    specs = {} if inputs is None else {"in_specs": [pl.BlockSpec(memory_space=at) for at in inputs]}
    return pl.pallas_call(
        kernel,
        out_shape=out_shapes,
        scratch_shapes=list(scratch),
        compiler_params=params(),
        **specs,
    )


def shape(dims, dtype):
    return jax.ShapeDtypeStruct(dims, dtype)


def one_hot(slots, k, capacity):
    tokens = slots.shape[1]
    return lax.broadcasted_iota(jnp.int32, (capacity, tokens), 0) == slots[k : k + 1, :]


def as_bf16(mask):
    return jnp.where(mask, 1.0, 0.0).astype(BF16)


def start_columns(source, target, sems):
    copies = []
    for at in range(0, target.shape[1], CHUNK):
        cols = pl.ds(at, CHUNK)
        copies.append(
            pltpu.make_async_copy(source.at[:, cols], target.at[:, cols], sems.at[at // CHUNK])
        )
        copies[-1].start()
    return copies


def dispatch_grads(count, ids_ref, gates_ref, grad_hbm, *refs):
    out_refs = refs[:count]
    slots_ref, table_ref, grad_ref, sems = refs[count:]
    width = grad_ref.shape[1]
    copies = start_columns(grad_hbm, grad_ref, sems)
    slots, first = slots_from(ids_ref[...])
    slots_ref[...] = slots
    gates = jnp.where(first, gates_ref[0:1, :], gates_ref[1:2, :])
    table_ref[...] = gates
    masks = [one_hot(slots, k, out_refs[k].shape[0]) for k in range(count)]
    picks = [as_bf16(mask) for mask in masks]
    scales = [
        jnp.sum(jnp.where(masks[k], gates[k : k + 1, :], 0.0), axis=1, keepdims=True)
        for k in range(count)
    ]
    for at in range(0, width, CHUNK):
        cols = slice(at, at + CHUNK)
        copies[at // CHUNK].wait()
        for k in range(count):
            rows = jnp.dot(picks[k], grad_ref[:, cols], preferred_element_type=F32)
            out_refs[k][:, cols] = (rows * scales[k]).astype(BF16)


def attend(parts, *refs):
    query_hbm, residual_hbm, gain_hbm, own_hbm = refs[0:4]
    other_refs = refs[4 : 3 + parts]
    stream_ref, left_ref, right_ref = refs[3 + parts : 6 + parts]
    query_ref, residual_ref, gain_ref, own_ref = refs[6 + parts : 10 + parts]
    query_sems, residual_sems, gain_sem, own_sem = refs[10 + parts :]
    tokens, width = query_ref.shape
    own_copy = pltpu.make_async_copy(own_hbm, own_ref, own_sem)
    own_copy.start()
    query_copies = start_columns(query_hbm, query_ref, query_sems)
    residual_copies = start_columns(residual_hbm, residual_ref, residual_sems)
    gain_copy = pltpu.make_async_copy(gain_hbm, gain_ref, gain_sem)
    gain_copy.start()
    memory_refs = (own_ref,) + tuple(other_refs)
    heads = GROUP // HEAD_SIZE
    rows = sum(ref.shape[1] for ref in memory_refs)
    own = (
        lax.broadcasted_iota(jnp.int32, (heads * rows, GROUP), 0) // rows
        == lax.broadcasted_iota(jnp.int32, (heads * rows, GROUP), 1) // HEAD_SIZE
    )
    total = jnp.zeros((tokens, 1), F32)

    def spread(which, cols):
        piece = jnp.concatenate([ref[which, :, cols] for ref in memory_refs], axis=0)
        return jnp.where(own, jnp.concatenate([piece] * heads, axis=0), jnp.zeros((), BF16))

    own_copy.wait()
    for at in range(0, width, GROUP):
        cols = slice(at, at + GROUP)
        if at % CHUNK == 0:
            query_copies[at // CHUNK].wait()
            residual_copies[at // CHUNK].wait()
        scores = lax.dot_general(
            spread(0, cols), query_ref[:, cols], (((1,), (1,)), ((), ())), preferred_element_type=F32
        ) * HEAD_SIZE ** (-0.5)
        scores = scores.reshape(heads, rows, tokens)
        exponent = jnp.exp(scores - jnp.max(scores, axis=1, keepdims=True))
        probs = exponent / jnp.sum(exponent, axis=1, keepdims=True)
        attended = lax.dot_general(
            probs.reshape(heads * rows, tokens).astype(BF16),
            spread(1, cols),
            (((0,), (0,)), ((), ())),
            preferred_element_type=F32,
        ).astype(BF16)
        stream = residual_ref[:, cols].astype(F32) + attended.astype(F32)
        stream_ref[:, cols] = stream
        total = total + jnp.sum(stream * stream, axis=1, keepdims=True)
    gain_copy.wait()
    scale = lax.rsqrt(total / width + 1e-06)
    half = width // 2
    for at in range(0, width, GROUP):
        cols = slice(at, at + GROUP)
        gain = gain_ref[cols].reshape(1, GROUP)
        piece = (stream_ref[:, cols] * scale * gain).astype(BF16)
        if at < half:
            left_ref[:, cols] = piece
        else:
            right_ref[:, at - half : at - half + GROUP] = piece


def slots_from(ids):
    tokens = ids.shape[1]
    me = lax.axis_index("expert")
    expert = lax.broadcasted_iota(jnp.int32, (8, tokens), 0) ^ me
    first = ids[0:1, :] == expert
    chosen = first | (ids[1:2, :] == expert)
    earlier = lax.broadcasted_iota(jnp.int32, (tokens, tokens), 0) < lax.broadcasted_iota(
        jnp.int32, (tokens, tokens), 1
    )
    count = jnp.dot(as_bf16(chosen), as_bf16(earlier), preferred_element_type=F32)
    return jnp.where(chosen, count.astype(jnp.int32), -1), first


def split_grads(ids_hbm, gates_hbm, grad_hbm, left_ref, right_ref, ids_ref, gates_ref, sems):
    tokens, half = grad_hbm.shape[0], left_ref.shape[1]
    copies = [
        pltpu.make_async_copy(ids_hbm, ids_ref, sems.at[0]),
        pltpu.make_async_copy(gates_hbm, gates_ref, sems.at[1]),
    ]
    for side, target in enumerate((left_ref, right_ref)):
        for part in range(2):
            rows = pl.ds(part * (tokens // 2), tokens // 2)
            copies.append(
                pltpu.make_async_copy(
                    grad_hbm.at[rows, pl.ds(side * half, half)],
                    target.at[rows, :],
                    sems.at[2 + 2 * side + part],
                )
            )
    for copy in copies:
        copy.start()
    copies[0].wait()
    copies[1].wait()
    gates = gates_ref[...]
    high = gates.astype(BF16).astype(F32)
    middle = (gates - high).astype(BF16).astype(F32)
    low = gates - high - middle
    notes = jnp.concatenate(
        [ids_ref[...].astype(F32), high, middle, low, jnp.zeros((8, tokens), F32)], axis=0
    ).astype(BF16)
    for target in (left_ref, right_ref):
        target[tokens:, :] = jnp.zeros((16, half), BF16)
        target[tokens:, 0:tokens] = notes
    for copy in copies[2:]:
        copy.wait()


def notes_of(ref):
    tokens = ref.shape[0] - 16
    notes = ref[tokens:, 0:tokens].astype(F32)
    slots, first = slots_from(notes[0:2].astype(jnp.int32))
    gates = notes[2:4] + notes[4:6] + notes[6:8]
    return slots, jnp.where(first, gates[0:1, :], gates[1:2, :])


def relay(ref, slots, gates, k, out_ref, place):
    tokens = slots.shape[1]
    capacity = out_ref.shape[0] // 2
    mask = one_hot(slots, k, capacity)
    pick = as_bf16(mask)
    if gates is not None:
        gate = jnp.sum(jnp.where(mask, gates[k : k + 1, :], 0.0), axis=1, keepdims=True)
    for at in range(0, ref.shape[1], GROUP):
        cols = slice(at, at + GROUP)
        rows = jnp.dot(pick, ref[0:tokens, cols], preferred_element_type=F32)
        if gates is not None:
            rows = rows * gate
        out_ref[place * capacity : (place + 1) * capacity, cols] = rows.astype(BF16)


def relay_grads(left_ref, right_ref, x_ref, y_ref, *refs):
    pass_left, pass_right, here_left, here_right, slots_ref, gates_ref = refs
    own, own_gates = notes_of(left_ref)
    by_x, x_gates = notes_of(x_ref)
    by_y, y_gates = notes_of(y_ref)
    slots_ref[0:8, :], slots_ref[8:16, :], slots_ref[16:24, :] = own, by_x, by_y
    gates_ref[...] = own_gates
    relay(left_ref, own, own_gates, 2, pass_left, 0)
    relay(x_ref, by_x, x_gates, 2, pass_left, 1)
    relay(right_ref, own, own_gates, 1, pass_right, 0)
    relay(y_ref, by_y, y_gates, 1, pass_right, 1)
    relay(left_ref, own, own_gates, 0, here_left, 0)
    relay(x_ref, by_x, x_gates, 0, here_left, 1)
    relay(right_ref, own, own_gates, 0, here_right, 0)
    relay(y_ref, by_y, y_gates, 0, here_right, 1)


def relay_rows(left_ref, right_ref, x_ref, y_ref, slots_ref, *refs):
    pass_left, pass_right, here_left, here_right = refs
    own, by_x, by_y = slots_ref[0:8, :], slots_ref[8:16, :], slots_ref[16:24, :]
    relay(left_ref, own, None, 2, pass_left, 0)
    relay(x_ref, by_x, None, 2, pass_left, 1)
    relay(right_ref, own, None, 1, pass_right, 0)
    relay(y_ref, by_y, None, 1, pass_right, 1)
    relay(left_ref, own, None, 0, here_left, 0)
    relay(x_ref, by_x, None, 0, here_left, 1)
    relay(right_ref, own, None, 0, here_right, 0)
    relay(y_ref, by_y, None, 0, here_right, 1)


def narrow(left_refs, right_refs, matrix_ref):
    half = matrix_ref.shape[1] // 2

    def product(ref, at):
        return lax.dot_general(
            ref[...], matrix_ref[:, at : at + half], (((1,), (1,)), ((), ())), preferred_element_type=F32
        )

    left = [product(ref, 0) for ref in left_refs]
    right = [product(ref, half) for ref in right_refs]
    size = left[0].shape[0] // 2
    low, high = slice(0, size), slice(size, 2 * size)
    return [
        left[0][low] + right[0][low],
        left[0][high] + right[1][low],
        left[1][low] + right[0][high],
        left[1][high] + right[1][high],
    ]


def back_products(*refs):
    parts = narrow(refs[0:2], refs[2:4], refs[4])
    refs[5][...] = jnp.concatenate(parts, axis=0)


def activate(value):
    square = value * value
    curve = jnp.tanh(GELU_C * (value + GELU_A * square * value))
    hidden = (0.5 * value * (1.0 + curve)).astype(BF16)
    slope = 0.5 * (1.0 + curve) + 0.5 * value * (1.0 - curve * curve) * (
        GELU_C * (1.0 + 3.0 * GELU_A * square)
    )
    return hidden, slope


def experts_of_four(*refs):
    in_ref, out_ref = refs[4:6]
    result_refs, slope_ref = refs[6:10], refs[10]
    hidden, slope = activate(jnp.concatenate(narrow(refs[0:2], refs[2:4], in_ref), axis=0))
    slope_ref[...] = slope
    size = result_refs[0].shape[0]
    for at in range(0, out_ref.shape[1], CHUNK):
        cols = slice(at, at + CHUNK)
        rows = jnp.dot(hidden, out_ref[:, cols], preferred_element_type=F32).astype(BF16)
        for k in range(4):
            result_refs[k][:, cols] = rows[k * size : (k + 1) * size]


def gradient_halves(left_refs, right_refs, back_ref, slope_ref):
    grads = (back_ref[...] * slope_ref[...]).astype(BF16)
    size = grads.shape[0] // 4
    swapped = jnp.concatenate(
        [grads[k * size : (k + 1) * size] for k in (0, 2, 1, 3)], axis=0
    )
    halves = []
    for refs, part in ((left_refs, grads), (right_refs, swapped)):
        rows = jnp.concatenate([ref[...] for ref in refs], axis=0)
        halves.append(
            lax.dot_general(rows, part, (((0,), (0,)), ((), ())), preferred_element_type=F32)
        )
    return halves


def four_packed(shards, *refs):
    keep_ref, send_ref = refs[6:]
    halves = gradient_halves(refs[0:2], refs[2:4], refs[4], refs[5])
    block = halves[0].shape[0] // shards
    core = lax.axis_index("seq")
    for shard in range(shards):
        full = halves[2 * shard // shards]
        at = (2 * shard) % shards * block
        even = pack(full[at : at + block])
        odd = pack(full[at + block : at + 2 * block])
        keep_ref[shard] = jnp.where(core == 0, even, odd)
        send_ref[shard] = jnp.where(core == 0, odd, even).astype(BF16)


def four_whole(*refs):
    halves = gradient_halves(refs[0:2], refs[2:4], refs[4], refs[5])
    half = halves[0].shape[0]
    refs[6][0:half, :] = halves[0]
    refs[6][half:, :] = halves[1]


def dispatch_rows(count, slots_ref, left_ref, right_ref, *out_refs):
    half = left_ref.shape[1]
    slots = slots_ref[...]
    for k in range(count):
        pick = as_bf16(one_hot(slots, k, out_refs[k].shape[0]))
        for at in range(0, half, GROUP):
            cols = slice(at, at + GROUP)
            there = slice(half + at, half + at + GROUP)
            out_refs[k][:, cols] = jnp.dot(
                pick, left_ref[:, cols], preferred_element_type=F32
            ).astype(BF16)
            out_refs[k][:, there] = jnp.dot(
                pick, right_ref[:, cols], preferred_element_type=F32
            ).astype(BF16)


def forward(rows_ref, in_ref, out_ref, result_ref):
    hidden, slope = activate(
        lax.dot_general(
            rows_ref[...], in_ref[...], (((1,), (1,)), ((), ())), preferred_element_type=F32
        )
    )
    for at in range(0, out_ref.shape[1], CHUNK):
        cols = slice(at, at + CHUNK)
        result_ref[:, cols] = jnp.dot(
            hidden, out_ref[:, cols], preferred_element_type=F32
        ).astype(BF16)
    return slope


def hidden_grad(grad_ref, out_ref):
    return lax.dot_general(
        grad_ref[...], out_ref[...], (((1,), (1,)), ((), ())), preferred_element_type=F32
    )


def expert_first(count, *refs):
    rows_refs, grad_refs = refs[0:count], refs[count : 2 * count + 1]
    in_ref, out_ref = refs[2 * count + 1 : 2 * count + 3]
    result_refs = refs[2 * count + 3 : 3 * count + 3]
    back_refs, last_ref = refs[3 * count + 3 : 4 * count + 3], refs[4 * count + 3]
    for k in range(count):
        slope = forward(rows_refs[k], in_ref, out_ref, result_refs[k])
        back_refs[k][...] = (hidden_grad(grad_refs[k], out_ref) * slope).astype(BF16)
    last_ref[...] = hidden_grad(grad_refs[count], out_ref)


def expert_last(rows_ref, back_ref, in_ref, out_ref, result_ref, grad_ref):
    slope = forward(rows_ref, in_ref, out_ref, result_ref)
    grad_ref[...] = (back_ref[...] * slope).astype(BF16)


def sum_of_products(rows_refs, grad_refs):
    rows = jnp.concatenate([ref[...] for ref in rows_refs], axis=0)
    grads = jnp.concatenate([ref[...] for ref in grad_refs], axis=0)
    return lax.dot_general(rows, grads, (((0,), (0,)), ((), ())), preferred_element_type=F32)


def pack(block):
    rows, columns = block.shape
    full = columns // 128 * 128
    pieces = [block[:, at : at + 128] for at in range(0, full, 128)]
    pieces.append(
        jnp.concatenate([block[: rows // 2, full:], block[rows // 2 :, full:]], axis=1)
    )
    return jnp.concatenate(pieces, axis=0)


def unpack(packed, rows, columns):
    full = columns // 128 * 128
    last = packed[full // 128 * rows :, :]
    half = columns - full
    pieces = [packed[at * rows : (at + 1) * rows, :] for at in range(full // 128)]
    pieces.append(jnp.concatenate([last[:, :half], last[:, half:]], axis=0))
    return jnp.concatenate(pieces, axis=1)


def weight_grads_whole(count, *refs):
    refs[2 * count][...] = sum_of_products(refs[0:count], refs[count : 2 * count])


def add_cores(shards, keep_ref, other_ref, own_ref, *send_refs):
    me = lax.axis_index("dp")
    own_ref[...] = keep_ref[me] + other_ref[me].astype(F32)
    for k in range(1, shards):
        send_refs[k - 1][...] = (keep_ref[me ^ k] + other_ref[me ^ k].astype(F32)).astype(BF16)


def add_replicas(own_ref, *refs):
    total = own_ref[...]
    for ref in refs[:-1]:
        total = total + ref[...].astype(F32)
    _, rows, columns = refs[-1].shape
    refs[-1][0] = unpack(total, rows, columns)


def combine(count, slots_ref, gates_ref, stream_ref, *refs):
    back_refs, out_ref = refs[0:count], refs[count]
    slots = slots_ref[0:8, :]
    gates = gates_ref[...].T
    width = stream_ref.shape[1]
    picks = [as_bf16(one_hot(slots, k, back_refs[k].shape[0])) for k in range(count)]
    for at in range(0, width, CHUNK):
        cols = slice(at, at + CHUNK)
        total = stream_ref[:, cols]
        for k in range(count):
            row = lax.dot_general(
                picks[k], back_refs[k][:, cols], (((0,), (0,)), ((), ())), preferred_element_type=F32
            )
            total = total + row * gates[:, k : k + 1]
        out_ref[:, cols] = total.astype(BF16)


def swap(value, axis, k):
    return lax.ppermute(value, axis, [(i, i ^ k) for i in range(lax.axis_size(axis))])


def per_device(
    queries, memory, residual, norm_gain, expert_ids, route_gates, weight_in, weight_out, layer_grad
):
    tokens, width = queries.shape
    hidden_width = weight_in.shape[2]
    experts, replicas, cores = (lax.axis_size(axis) for axis in ("expert", "dp", "seq"))
    capacity = (5 * tokens + 2 * experts - 1) // (2 * experts)
    capacity = (capacity + 15) // 16 * 16
    half = width // 2
    in_hbm = functools.partial(pltpu.with_memory_space_constraint, memory_space=pltpu.HBM)
    ids, gates = in_hbm(expert_ids.T), in_hbm(route_gates.T)
    layer_grad, queries, residual = in_hbm(layer_grad), in_hbm(queries), in_hbm(residual)
    matrix_in, matrix_out = weight_in[0].T, weight_out[0]
    table = shape((8, tokens), F32)
    vmem, hbm = pltpu.VMEM, pltpu.HBM

    if cores == 2:
        memories = [swap(memory, "seq", 1)]
        own_memory = in_hbm(memory)
    else:
        memories = []
        own_memory = in_hbm(lax.all_gather(memory, "seq", axis=1, tiled=True))
    parts = 1 + len(memories)
    dma = pltpu.SemaphoreType.DMA
    attend_call = call(
        functools.partial(attend, parts),
        [shape((tokens, width), F32)] + [shape((tokens, half), BF16)] * 2,
        [vmem((tokens, width), BF16)] * 2
        + [vmem((width,), F32), vmem(own_memory.shape, BF16)]
        + [dma((width // CHUNK,))] * 2
        + [dma, dma],
        [hbm] * 4 + [vmem] * len(memories),
    )
    attend_inputs = (queries, residual, in_hbm(norm_gain), own_memory, *memories)

    if experts == 4:
        with_notes = shape((tokens + 16, half), BF16)
        pairs = shape((2 * capacity, half), BF16)
        narrow_shape = shape((4 * capacity, hidden_width), F32)
        left_grad, right_grad = call(
            split_grads,
            [with_notes] * 2,
            [vmem((2, tokens), jnp.int32), vmem((2, tokens), F32), dma((6,))],
            [hbm] * 3,
        )(ids, gates, layer_grad)
        x_grad, y_grad = swap(left_grad, "expert", 1), swap(right_grad, "expert", 2)
        stream, left, right = attend_call(*attend_inputs)
        x_rows, y_rows = swap(left, "expert", 1), swap(right, "expert", 2)
        pass_left, pass_right, here_left, here_right, slots, gates = call(
            relay_grads, [pairs] * 4 + [shape((24, tokens), jnp.int32), table]
        )(left_grad, right_grad, x_grad, y_grad)
        grads = (
            here_left,
            swap(pass_left, "expert", 2),
            here_right,
            swap(pass_right, "expert", 1),
        )
        pass_left, pass_right, here_left, here_right = call(relay_rows, [pairs] * 4)(
            left, right, x_rows, y_rows, slots
        )
        rows = (
            here_left,
            swap(pass_left, "expert", 2),
            here_right,
            swap(pass_right, "expert", 1),
        )
        back = call(back_products, narrow_shape)(*grads, matrix_out)
        *results, slope = call(
            experts_of_four, [shape((capacity, width), BF16)] * 4 + [narrow_shape]
        )(*rows, matrix_in, matrix_out)
        products = (*rows, back, slope)
        whole_call = four_whole
    else:
        rows_shape = [shape((capacity, width), BF16)] * experts
        *grads, slots, gates = call(
            functools.partial(dispatch_grads, experts),
            rows_shape + [shape((8, tokens), jnp.int32), table],
            [vmem((tokens, width), BF16), dma((width // CHUNK,))],
            [vmem, vmem, hbm],
        )(expert_ids.T, route_gates.T, layer_grad)
        grads = [grads[0]] + [swap(grads[k], "expert", k) for k in range(1, experts)]
        stream, left, right = attend_call(*attend_inputs)
        rows = call(functools.partial(dispatch_rows, experts), rows_shape)(slots, left, right)
        rows = [rows[0]] + [swap(rows[k], "expert", k) for k in range(1, experts)]
        last = experts - 1
        back_shape = shape((capacity, hidden_width), BF16)
        outs = call(
            functools.partial(expert_first, last),
            rows_shape[:last] + [back_shape] * last + [shape((capacity, hidden_width), F32)],
        )(*rows[:last], *grads, matrix_in, matrix_out)
        result, back = call(expert_last, [rows_shape[0], back_shape])(
            rows[last], outs[2 * last], matrix_in, matrix_out
        )
        results = list(outs[:last]) + [result]
        products = (*rows, *outs[last : 2 * last], back)
        whole_call = functools.partial(weight_grads_whole, experts)
    results = [results[0]] + [swap(results[k], "expert", k) for k in range(1, experts)]

    block = width // (replicas * cores)
    if experts == 4 and cores == 2 and replicas == 4 and block % 32 == 0 and hidden_width % 128 == 64:
        packed = (replicas, block * hidden_width // 128, 128)
        keep, send = call(
            functools.partial(four_packed, replicas), [shape(packed, F32), shape(packed, BF16)]
        )(*products)
        own, *sends = call(
            functools.partial(add_cores, replicas),
            [shape(packed[1:], F32)] + [shape(packed[1:], BF16)] * (replicas - 1),
        )(keep, swap(send, "seq", 1))
        received = [swap(sends[k - 1], "dp", k) for k in range(1, replicas)]
        grads_here = call(add_replicas, shape((1, block, hidden_width), F32))(own, *received)
    else:
        whole = call(whole_call, shape((width, hidden_width), F32))(*products)
        grads_here = lax.psum_scatter(whole, ("dp", "seq"), scatter_dimension=0, tiled=True)[None]

    layer_output = call(functools.partial(combine, experts), shape((tokens, width), BF16))(
        slots, gates, stream, *results
    )
    return layer_output, grads_here


def solution(mesh):
    rows = P(("dp", "expert", "seq"), None)
    return jax.shard_map(
        per_device,
        mesh=mesh,
        in_specs=(
            rows,
            P(None, ("dp", "expert", "seq"), None),
            rows,
            P(),
            rows,
            rows,
            P("expert", None, None),
            P("expert", None, None),
            rows,
        ),
        out_specs=(rows, P("expert", ("dp", "seq"), None)),
        check_vma=False,
    )
```

```python
import functools

import jax
import jax.numpy as jnp
from jax import lax
from jax.experimental import pallas as pl
from jax.experimental.pallas import tpu as pltpu
from jax.sharding import PartitionSpec as P

HEAD_SIZE = 64
GROUP = 256
CHUNK = 512
VMEM_LIMIT = 24 * 1024 * 1024
GELU_C = 0.7978845608028654
GELU_A = 0.044715
BF16 = jnp.bfloat16
F32 = jnp.float32


def params():
    return pltpu.CompilerParams(vmem_limit_bytes=VMEM_LIMIT)


def call(kernel, out_shapes, scratch=(), inputs=None):
    specs = {} if inputs is None else {"in_specs": [pl.BlockSpec(memory_space=at) for at in inputs]}
    return pl.pallas_call(
        kernel,
        out_shape=out_shapes,
        scratch_shapes=list(scratch),
        compiler_params=params(),
        **specs,
    )


def shape(dims, dtype):
    return jax.ShapeDtypeStruct(dims, dtype)


def one_hot(slots, k, capacity):
    tokens = slots.shape[1]
    return lax.broadcasted_iota(jnp.int32, (capacity, tokens), 0) == slots[k : k + 1, :]


def as_bf16(mask):
    return jnp.where(mask, 1.0, 0.0).astype(BF16)


def start_columns(source, target, sems):
    copies = []
    for at in range(0, target.shape[1], CHUNK):
        cols = pl.ds(at, CHUNK)
        copies.append(
            pltpu.make_async_copy(source.at[:, cols], target.at[:, cols], sems.at[at // CHUNK])
        )
        copies[-1].start()
    return copies


def dispatch_grads(count, ids_ref, gates_ref, grad_hbm, *refs):
    out_refs = refs[:count]
    slots_ref, table_ref, grad_ref, sems = refs[count:]
    width = grad_ref.shape[1]
    copies = start_columns(grad_hbm, grad_ref, sems)
    slots, first = slots_from(ids_ref[...])
    slots_ref[...] = slots
    gates = jnp.where(first, gates_ref[0:1, :], gates_ref[1:2, :])
    table_ref[...] = gates
    masks = [one_hot(slots, k, out_refs[k].shape[0]) for k in range(count)]
    picks = [as_bf16(mask) for mask in masks]
    scales = [
        jnp.sum(jnp.where(masks[k], gates[k : k + 1, :], 0.0), axis=1, keepdims=True)
        for k in range(count)
    ]
    for at in range(0, width, CHUNK):
        cols = slice(at, at + CHUNK)
        copies[at // CHUNK].wait()
        for k in range(count):
            rows = jnp.dot(picks[k], grad_ref[:, cols], preferred_element_type=F32)
            out_refs[k][:, cols] = (rows * scales[k]).astype(BF16)


def attend(parts, hops, slots_ref, *refs):
    query_hbm, residual_hbm, gain_hbm = refs[0:3]
    memory_refs = refs[3 : 3 + parts]
    stream_ref, left_ref, right_ref = refs[3 + parts : 6 + parts]
    query_ref, residual_ref, gain_ref = refs[6 + parts : 9 + parts]
    query_sems, residual_sems, gain_sem = refs[9 + parts :]
    tokens, width = query_ref.shape
    query_copies = start_columns(query_hbm, query_ref, query_sems)
    residual_copies = start_columns(residual_hbm, residual_ref, residual_sems)
    gain_copy = pltpu.make_async_copy(gain_hbm, gain_ref, gain_sem)
    gain_copy.start()
    heads = GROUP // HEAD_SIZE
    rows = sum(ref.shape[1] for ref in memory_refs)
    own = (
        lax.broadcasted_iota(jnp.int32, (heads * rows, GROUP), 0) // rows
        == lax.broadcasted_iota(jnp.int32, (heads * rows, GROUP), 1) // HEAD_SIZE
    )
    total = jnp.zeros((tokens, 1), F32)

    def spread(which, cols):
        piece = jnp.concatenate([ref[which, :, cols] for ref in memory_refs], axis=0)
        return jnp.where(own, jnp.concatenate([piece] * heads, axis=0), jnp.zeros((), BF16))

    for at in range(0, width, GROUP):
        cols = slice(at, at + GROUP)
        if at % CHUNK == 0:
            query_copies[at // CHUNK].wait()
            residual_copies[at // CHUNK].wait()
        scores = lax.dot_general(
            spread(0, cols), query_ref[:, cols], (((1,), (1,)), ((), ())), preferred_element_type=F32
        ) * HEAD_SIZE ** (-0.5)
        scores = scores.reshape(heads, rows, tokens)
        exponent = jnp.exp(scores - jnp.max(scores, axis=1, keepdims=True))
        probs = exponent / jnp.sum(exponent, axis=1, keepdims=True)
        attended = lax.dot_general(
            probs.reshape(heads * rows, tokens).astype(BF16),
            spread(1, cols),
            (((0,), (0,)), ((), ())),
            preferred_element_type=F32,
        ).astype(BF16)
        stream = residual_ref[:, cols].astype(F32) + attended.astype(F32)
        stream_ref[:, cols] = stream
        total = total + jnp.sum(stream * stream, axis=1, keepdims=True)
    gain_copy.wait()
    scale = lax.rsqrt(total / width + 1e-06)
    half = width // 2
    for at in range(0, width, GROUP):
        cols = slice(at, at + GROUP)
        gain = gain_ref[cols].reshape(1, GROUP)
        piece = (stream_ref[:, cols] * scale * gain).astype(BF16)
        if at < half:
            left_ref[0:tokens, cols] = piece
        else:
            right_ref[0:tokens, at - half : at - half + GROUP] = piece
    if hops:
        slots = slots_ref[...]
        relay(right_ref, slots, None, 1, left_ref, slice(tokens, None))
        relay(left_ref, slots, None, 2, right_ref, slice(tokens, None))


def slots_from(ids):
    tokens = ids.shape[1]
    me = lax.axis_index("expert")
    expert = lax.broadcasted_iota(jnp.int32, (8, tokens), 0) ^ me
    first = ids[0:1, :] == expert
    chosen = first | (ids[1:2, :] == expert)
    earlier = lax.broadcasted_iota(jnp.int32, (tokens, tokens), 0) < lax.broadcasted_iota(
        jnp.int32, (tokens, tokens), 1
    )
    count = jnp.dot(as_bf16(chosen), as_bf16(earlier), preferred_element_type=F32)
    return jnp.where(chosen, count.astype(jnp.int32), -1), first


def split_grads(ids_hbm, gates_hbm, grad_hbm, memory_hbm, *refs):
    left_ref, right_ref, slots_ref, table_ref, memory_ref, ids_ref, gates_ref, sems = refs
    tokens, half = grad_hbm.shape[0], left_ref.shape[1]
    copies = [
        pltpu.make_async_copy(ids_hbm, ids_ref, sems.at[0]),
        pltpu.make_async_copy(gates_hbm, gates_ref, sems.at[1]),
        pltpu.make_async_copy(memory_hbm, memory_ref, sems.at[6]),
    ]
    for side, target in enumerate((left_ref, right_ref)):
        for part in range(2):
            rows = pl.ds(part * (tokens // 2), tokens // 2)
            copies.append(
                pltpu.make_async_copy(
                    grad_hbm.at[rows, pl.ds(side * half, half)],
                    target.at[rows, :],
                    sems.at[2 + 2 * side + part],
                )
            )
    for copy in copies:
        copy.start()
    copies[0].wait()
    copies[1].wait()
    gates = gates_ref[...]
    high = gates.astype(BF16).astype(F32)
    middle = (gates - high).astype(BF16).astype(F32)
    low = gates - high - middle
    notes = jnp.concatenate(
        [ids_ref[...].astype(F32), high, middle, low, jnp.zeros((8, tokens), F32)], axis=0
    ).astype(BF16)
    for target in (left_ref, right_ref):
        target[tokens : tokens + 16, :] = jnp.zeros((16, half), BF16)
        target[tokens : tokens + 16, 0:tokens] = notes
    slots, first = slots_from(ids_ref[...])
    table = jnp.where(first, gates[0:1, :], gates[1:2, :])
    slots_ref[...], table_ref[...] = slots, table
    for copy in copies[2:]:
        copy.wait()
    relay(right_ref, slots, table, 1, left_ref, slice(tokens + 16, None))
    relay(left_ref, slots, table, 2, right_ref, slice(tokens + 16, None))


def notes_of(ref, tokens):
    notes = ref[tokens : tokens + 16, 0:tokens].astype(F32)
    slots, first = slots_from(notes[0:2].astype(jnp.int32))
    gates = notes[2:4] + notes[4:6] + notes[6:8]
    return slots, jnp.where(first, gates[0:1, :], gates[1:2, :])


def relay(ref, slots, gates, k, out_ref, place, shift=0):
    tokens = slots.shape[1]
    rows_at = range(*place.indices(out_ref.shape[0]))
    mask = one_hot(slots, k, len(rows_at))
    pick = as_bf16(mask)
    if gates is not None:
        gate = jnp.sum(jnp.where(mask, gates[k : k + 1, :], 0.0), axis=1, keepdims=True)
    for at in range(0, ref.shape[1], GROUP):
        rows = jnp.dot(pick, ref[0:tokens, at : at + GROUP], preferred_element_type=F32)
        if gates is not None:
            rows = rows * gate
        out_ref[place, shift + at : shift + at + GROUP] = rows.astype(BF16)


def gather_near(own, by_x, by_y, blocks, direct, near_ref):
    (own_slots, own_gates), (x_slots, x_gates), (y_slots, y_gates) = own, by_x, by_y
    left_ref, right_ref, x_ref, y_ref = blocks
    capacity, half = near_ref.shape[0] // 3, left_ref.shape[1]
    here, at_x, at_y = (slice(k * capacity, (k + 1) * capacity) for k in range(3))
    relay(left_ref, own_slots, own_gates, 0, near_ref, here)
    relay(right_ref, own_slots, own_gates, 0, near_ref, here, half)
    relay(x_ref, x_slots, x_gates, 0, near_ref, at_x)
    near_ref[at_x, half:] = x_ref[direct, :]
    near_ref[at_y, 0:half] = y_ref[direct, :]
    relay(y_ref, y_slots, y_gates, 0, near_ref, at_y, half)


def relay_grads(left_ref, right_ref, x_ref, y_ref, slots_ref, table_ref, *refs):
    pass_left, pass_right, near_ref, others_ref = refs
    tokens = slots_ref.shape[1]
    x_notes, y_notes = notes_of(x_ref, tokens), notes_of(y_ref, tokens)
    others_ref[0:8, :], others_ref[8:16, :] = x_notes[0], y_notes[0]
    relay(x_ref, *x_notes, 2, pass_left, slice(None))
    relay(y_ref, *y_notes, 1, pass_right, slice(None))
    blocks = (left_ref, right_ref, x_ref, y_ref)
    own = (slots_ref[...], table_ref[...])
    gather_near(own, x_notes, y_notes, blocks, slice(tokens + 16, None), near_ref)


def relay_rows(left_ref, right_ref, x_ref, y_ref, slots_ref, others_ref, *refs):
    pass_left, pass_right, near_ref = refs
    by_x, by_y = (others_ref[0:8, :], None), (others_ref[8:16, :], None)
    relay(x_ref, *by_x, 2, pass_left, slice(None))
    relay(y_ref, *by_y, 1, pass_right, slice(None))
    blocks = (left_ref, right_ref, x_ref, y_ref)
    direct = slice(slots_ref.shape[1], None)
    gather_near((slots_ref[...], None), by_x, by_y, blocks, direct, near_ref)


def activate(value):
    square = value * value
    curve = jnp.tanh(GELU_C * (value + GELU_A * square * value))
    hidden = (0.5 * value * (1.0 + curve)).astype(BF16)
    slope = 0.5 * (1.0 + curve) + 0.5 * value * (1.0 - curve * curve) * (
        GELU_C * (1.0 + 3.0 * GELU_A * square)
    )
    return hidden, slope


def narrow(left_ref, right_ref, matrix_ref):
    half = left_ref.shape[1]
    return sum(
        lax.dot_general(
            ref[...], matrix_ref[:, at : at + half], (((1,), (1,)), ((), ())), preferred_element_type=F32
        )
        for ref, at in ((left_ref, 0), (right_ref, half))
    )


def back_products(near_ref, left_ref, right_ref, out_ref, near_back_ref, far_back_ref):
    near_back_ref[...] = hidden_grad(near_ref, out_ref)
    far_back_ref[...] = narrow(left_ref, right_ref, out_ref)


def experts_near(near_ref, back_ref, in_ref, out_ref, *refs):
    result_refs, grad_ref = refs[0:3], refs[3]
    hidden, slope = activate(hidden_grad(near_ref, in_ref))
    grad_ref[...] = (back_ref[...] * slope).astype(BF16)
    size = result_refs[0].shape[0]
    for at in range(0, out_ref.shape[1], CHUNK):
        cols = slice(at, at + CHUNK)
        rows = jnp.dot(hidden, out_ref[:, cols], preferred_element_type=F32).astype(BF16)
        for k in range(3):
            result_refs[k][:, cols] = rows[k * size : (k + 1) * size]


def weight_grads_near(near_ref, grad_ref, total_ref):
    total_ref[...] = lax.dot_general(
        near_ref[...], grad_ref[...], (((0,), (0,)), ((), ())), preferred_element_type=F32
    )


def finish_far(shards, *refs):
    left_ref, right_ref, back_ref, in_ref, total_ref = refs[0:5]
    hidden_ref, keep_ref, send_ref = refs[5:]

    hidden, slope = activate(narrow(left_ref, right_ref, in_ref))
    hidden_ref[...] = hidden
    grads = (back_ref[...] * slope).astype(BF16)
    halves = [
        lax.dot_general(ref[...], grads, (((0,), (0,)), ((), ())), preferred_element_type=F32)
        for ref in (left_ref, right_ref)
    ]
    block = total_ref.shape[0] // (2 * shards)
    core = lax.axis_index("seq")
    for shard in range(shards):
        full = halves[2 * shard // shards]
        at, there = (2 * shard) % shards * block, 2 * shard * block
        even = pack(full[at : at + block] + total_ref[there : there + block, :])
        odd = pack(
            full[at + block : at + 2 * block] + total_ref[there + block : there + 2 * block, :]
        )
        keep_ref[shard] = jnp.where(core == 0, even, odd)
        send_ref[shard] = jnp.where(core == 0, odd, even).astype(BF16)


def widen(hidden_ref, out_ref, result_ref):
    for at in range(0, out_ref.shape[1], CHUNK):
        cols = slice(at, at + CHUNK)
        result_ref[:, cols] = jnp.dot(
            hidden_ref[...], out_ref[:, cols], preferred_element_type=F32
        ).astype(BF16)


def dispatch_rows(count, slots_ref, left_ref, right_ref, *out_refs):
    half = left_ref.shape[1]
    slots = slots_ref[...]
    for k in range(count):
        pick = as_bf16(one_hot(slots, k, out_refs[k].shape[0]))
        for at in range(0, half, GROUP):
            cols = slice(at, at + GROUP)
            there = slice(half + at, half + at + GROUP)
            out_refs[k][:, cols] = jnp.dot(
                pick, left_ref[:, cols], preferred_element_type=F32
            ).astype(BF16)
            out_refs[k][:, there] = jnp.dot(
                pick, right_ref[:, cols], preferred_element_type=F32
            ).astype(BF16)


def forward(rows_ref, in_ref, out_ref, result_ref):
    hidden, slope = activate(
        lax.dot_general(
            rows_ref[...], in_ref[...], (((1,), (1,)), ((), ())), preferred_element_type=F32
        )
    )
    for at in range(0, out_ref.shape[1], CHUNK):
        cols = slice(at, at + CHUNK)
        result_ref[:, cols] = jnp.dot(
            hidden, out_ref[:, cols], preferred_element_type=F32
        ).astype(BF16)
    return slope


def hidden_grad(grad_ref, out_ref):
    return lax.dot_general(
        grad_ref[...], out_ref[...], (((1,), (1,)), ((), ())), preferred_element_type=F32
    )


def expert_first(count, *refs):
    rows_refs, grad_refs = refs[0:count], refs[count : 2 * count + 1]
    in_ref, out_ref = refs[2 * count + 1 : 2 * count + 3]
    result_refs = refs[2 * count + 3 : 3 * count + 3]
    back_refs, last_ref = refs[3 * count + 3 : 4 * count + 3], refs[4 * count + 3]
    for k in range(count):
        slope = forward(rows_refs[k], in_ref, out_ref, result_refs[k])
        back_refs[k][...] = (hidden_grad(grad_refs[k], out_ref) * slope).astype(BF16)
    last_ref[...] = hidden_grad(grad_refs[count], out_ref)


def expert_last(rows_ref, back_ref, in_ref, out_ref, result_ref, grad_ref):
    slope = forward(rows_ref, in_ref, out_ref, result_ref)
    grad_ref[...] = (back_ref[...] * slope).astype(BF16)


def sum_of_products(rows_refs, grad_refs):
    rows = jnp.concatenate([ref[...] for ref in rows_refs], axis=0)
    grads = jnp.concatenate([ref[...] for ref in grad_refs], axis=0)
    return lax.dot_general(rows, grads, (((0,), (0,)), ((), ())), preferred_element_type=F32)


def pack(block):
    rows, columns = block.shape
    full = columns // 128 * 128
    pieces = [block[:, at : at + 128] for at in range(0, full, 128)]
    pieces.append(
        jnp.concatenate([block[: rows // 2, full:], block[rows // 2 :, full:]], axis=1)
    )
    return jnp.concatenate(pieces, axis=0)


def unpack(packed, rows, columns):
    full = columns // 128 * 128
    last = packed[full // 128 * rows :, :]
    half = columns - full
    pieces = [packed[at * rows : (at + 1) * rows, :] for at in range(full // 128)]
    pieces.append(jnp.concatenate([last[:, :half], last[:, half:]], axis=0))
    return jnp.concatenate(pieces, axis=1)


def weight_grads_whole(count, *refs):
    refs[2 * count][...] = sum_of_products(refs[0:count], refs[count : 2 * count])


def add_cores(keep_ref, other_ref, own_ref, *sum_refs):
    me = lax.axis_index("dp")
    own_ref[...] = keep_ref[me] + other_ref[me].astype(F32)
    for k, sum_ref in enumerate(sum_refs):
        sum_ref[...] = (keep_ref[me ^ (3 - k)] + other_ref[me ^ (3 - k)].astype(F32)).astype(BF16)


def combine_here(slots_ref, gates_ref, stream_ref, here_ref, total_ref):
    mix_into(slots_ref, gates_ref, (0,), stream_ref, (here_ref,), total_ref)


def finish(*refs):
    slots_ref, gates_ref, base_ref, x_ref, y_ref, far_ref = refs[0:6]
    out_hbm, sum_hbm, out_ref, sum_ref, sems, sum_sem = refs[10:]
    total = refs[6][...]
    for ref in refs[7:10]:
        total = total + ref[...].astype(F32)
    _, rows, columns = sum_ref.shape
    sum_ref[0] = unpack(total, rows, columns)
    copies = [pltpu.make_async_copy(sum_ref, sum_hbm, sum_sem)]
    copies[0].start()

    def send(cols):
        at = cols.start
        copy = pltpu.make_async_copy(
            out_ref.at[:, pl.ds(at, CHUNK)], out_hbm.at[:, pl.ds(at, CHUNK)], sems.at[at // CHUNK]
        )
        copy.start()
        copies.append(copy)

    mix_into(
        slots_ref, gates_ref, (1, 2, 3), base_ref, (x_ref, y_ref, far_ref), out_ref, send
    )
    for copy in copies:
        copy.wait()


def mix_into(slots_ref, gates_ref, sources, base_ref, result_refs, out_ref, after=None):
    slots = slots_ref[...]
    gates = gates_ref[...].T
    picks = [as_bf16(one_hot(slots, k, ref.shape[0])) for k, ref in zip(sources, result_refs)]
    for at in range(0, base_ref.shape[1], CHUNK):
        cols = slice(at, at + CHUNK)
        total = base_ref[:, cols]
        for k, pick, ref in zip(sources, picks, result_refs):
            row = lax.dot_general(
                pick, ref[:, cols], (((0,), (0,)), ((), ())), preferred_element_type=F32
            )
            total = total + row * gates[:, k : k + 1]
        out_ref[:, cols] = total.astype(out_ref.dtype)
        if after is not None:
            after(cols)


def combine(count, slots_ref, gates_ref, stream_ref, *refs):
    mix_into(slots_ref, gates_ref, range(count), stream_ref, refs[0:count], refs[count])


def swap(value, axis, k):
    return lax.ppermute(value, axis, [(i, i ^ k) for i in range(lax.axis_size(axis))])


def per_device(
    queries, memory, residual, norm_gain, expert_ids, route_gates, weight_in, weight_out, layer_grad
):
    tokens, width = queries.shape
    hidden_width = weight_in.shape[2]
    experts, replicas, cores = (lax.axis_size(axis) for axis in ("expert", "dp", "seq"))
    capacity = (5 * tokens + 2 * experts - 1) // (2 * experts)
    capacity = (capacity + 15) // 16 * 16
    half = width // 2
    in_hbm = functools.partial(pltpu.with_memory_space_constraint, memory_space=pltpu.HBM)
    ids, gates = in_hbm(expert_ids.T), in_hbm(route_gates.T)
    layer_grad, queries, residual = in_hbm(layer_grad), in_hbm(queries), in_hbm(residual)
    matrix_in, matrix_out = weight_in[0].T, weight_out[0]
    table = shape((8, tokens), F32)
    vmem, hbm = pltpu.VMEM, pltpu.HBM

    own_memory = in_hbm(memory) if cores == 2 else lax.all_gather(memory, "seq", axis=1, tiled=True)
    parts = cores if cores == 2 else 1
    dma = pltpu.SemaphoreType.DMA
    block = width // (replicas * cores)
    hops = experts == 4 and cores == 2 and replicas == 4 and block % 32 == 0
    hops = hops and hidden_width % 128 == 64
    extra = capacity if hops else 0
    attend_call = call(
        functools.partial(attend, parts, hops),
        [shape((tokens, width), F32)] + [shape((tokens + extra, half), BF16)] * 2,
        [vmem((tokens, width), BF16)] * 2
        + [vmem((width,), F32)]
        + [dma((width // CHUNK,))] * 2
        + [dma],
        [vmem] + [hbm] * 3 + [vmem] * parts,
    )
    attend_inputs = (queries, residual, in_hbm(norm_gain))
    integers = shape((8, tokens), jnp.int32)

    if hops:
        first_hop = shape((tokens + 16 + capacity, half), BF16)
        second_hop = shape((capacity, half), BF16)
        near = shape((3 * capacity, width), BF16)
        near_narrow = (3 * capacity, hidden_width)
        left, right, slots, gates, own_memory = call(
            split_grads,
            [first_hop] * 2 + [integers, table, shape(memory.shape, BF16)],
            [vmem((2, tokens), jnp.int32), vmem((2, tokens), F32), dma((7,))],
            [hbm] * 4,
        )(ids, gates, layer_grad, own_memory)
        by_x, by_y = swap(left, "expert", 1), swap(right, "expert", 2)
        stream, left_rows, right_rows = attend_call(
            slots, *attend_inputs, own_memory, swap(own_memory, "seq", 1)
        )
        rows_x, rows_y = swap(left_rows, "expert", 1), swap(right_rows, "expert", 2)
        pass_left, pass_right, near_grads, others = call(
            relay_grads, [second_hop] * 2 + [near, shape((16, tokens), jnp.int32)]
        )(left, right, by_x, by_y, slots, gates)
        far_grads = (swap(pass_left, "expert", 2), swap(pass_right, "expert", 1))
        pass_left, pass_right, near_rows = call(relay_rows, [second_hop] * 2 + [near])(
            left_rows, right_rows, rows_x, rows_y, slots, others
        )
        far_rows = (swap(pass_left, "expert", 2), swap(pass_right, "expert", 1))
        back, far_back = call(
            back_products, [shape(near_narrow, F32), shape((capacity, hidden_width), F32)]
        )(near_grads, *far_grads, matrix_out)
        result_shape = shape((capacity, width), BF16)
        *results, near_pre = call(experts_near, [result_shape] * 3 + [shape(near_narrow, BF16)])(
            near_rows, back, matrix_in, matrix_out
        )
        total = call(weight_grads_near, shape((width, hidden_width), F32))(near_rows, near_pre)
        packed = (replicas, block * hidden_width // 128, 128)
        hidden, keep, send = call(
            functools.partial(finish_far, replicas),
            [shape((capacity, hidden_width), BF16), shape(packed, F32), shape(packed, BF16)],
        )(*far_rows, far_back, matrix_in, total)
        here, from_x, from_y = [results[0]] + [swap(results[k], "expert", k) for k in (1, 2)]
        far = swap(call(widen, result_shape)(hidden, matrix_out), "expert", 3)
        one = shape(packed[1:], BF16)
        own, *sums = call(add_cores, [shape(packed[1:], F32), one, one, one])(
            keep, swap(send, "seq", 1)
        )
        received = [swap(part, "dp", 3 - k) for k, part in enumerate(sums)]
        base = call(combine_here, shape((tokens, width), F32))(slots, gates, stream, here)
        grads_shape = (1, block, hidden_width)
        layer_output, grads_here = pl.pallas_call(
            finish,
            out_shape=[shape((tokens, width), BF16), shape(grads_shape, F32)],
            in_specs=[pl.BlockSpec(memory_space=vmem)] * 10,
            out_specs=[pl.BlockSpec(memory_space=hbm)] * 2,
            scratch_shapes=[
                vmem((tokens, width), BF16),
                vmem(grads_shape, F32),
                dma((width // CHUNK,)),
                dma,
            ],
            compiler_params=params(),
        )(slots, gates, base, from_x, from_y, far, own, *received)
    else:
        rows_shape = [shape((capacity, width), BF16)] * experts
        *grads, slots, gates = call(
            functools.partial(dispatch_grads, experts),
            rows_shape + [integers, table],
            [vmem((tokens, width), BF16), dma((width // CHUNK,))],
            [vmem, vmem, hbm],
        )(expert_ids.T, route_gates.T, layer_grad)
        grads = [grads[0]] + [swap(grads[k], "expert", k) for k in range(1, experts)]
        memories = [own_memory] if cores != 2 else [own_memory, swap(own_memory, "seq", 1)]
        stream, left, right = attend_call(slots, *attend_inputs, *memories)
        rows = call(functools.partial(dispatch_rows, experts), rows_shape)(slots, left, right)
        rows = [rows[0]] + [swap(rows[k], "expert", k) for k in range(1, experts)]
        last = experts - 1
        back_shape = shape((capacity, hidden_width), BF16)
        outs = call(
            functools.partial(expert_first, last),
            rows_shape[:last] + [back_shape] * last + [shape((capacity, hidden_width), F32)],
        )(*rows[:last], *grads, matrix_in, matrix_out)
        result, back = call(expert_last, [rows_shape[0], back_shape])(
            rows[last], outs[2 * last], matrix_in, matrix_out
        )
        results = list(outs[:last]) + [result]
        whole = call(
            functools.partial(weight_grads_whole, experts), shape((width, hidden_width), F32)
        )(*rows, *outs[last : 2 * last], back)
        grads_here = lax.psum_scatter(whole, ("dp", "seq"), scatter_dimension=0, tiled=True)[None]
        results = [results[0]] + [swap(results[k], "expert", k) for k in range(1, experts)]
        layer_output = call(functools.partial(combine, experts), shape((tokens, width), BF16))(
            slots, gates, stream, *results
        )
    return layer_output, grads_here


def solution(mesh):
    rows = P(("dp", "expert", "seq"), None)
    return jax.shard_map(
        per_device,
        mesh=mesh,
        in_specs=(
            rows,
            P(None, ("dp", "expert", "seq"), None),
            rows,
            P(),
            rows,
            rows,
            P("expert", None, None),
            P("expert", None, None),
            rows,
        ),
        out_specs=(rows, P("expert", ("dp", "seq"), None)),
        check_vma=False,
    )
```

```python
import functools

import jax
import jax.numpy as jnp
from jax import lax
from jax.experimental import pallas as pl
from jax.experimental.pallas import tpu as pltpu
from jax.sharding import PartitionSpec as P

HEAD_SIZE = 64
GROUP = 256
CHUNK = 512
VMEM_LIMIT = 24 * 1024 * 1024
GELU_C = 0.7978845608028654
GELU_A = 0.044715
BF16 = jnp.bfloat16
F32 = jnp.float32


def params():
    return pltpu.CompilerParams(vmem_limit_bytes=VMEM_LIMIT)


def call(kernel, out_shapes, scratch=(), inputs=None):
    specs = {} if inputs is None else {"in_specs": [pl.BlockSpec(memory_space=at) for at in inputs]}
    return pl.pallas_call(
        kernel,
        out_shape=out_shapes,
        scratch_shapes=list(scratch),
        compiler_params=params(),
        **specs,
    )


def shape(dims, dtype):
    return jax.ShapeDtypeStruct(dims, dtype)


def one_hot(slots, k, capacity):
    tokens = slots.shape[1]
    return lax.broadcasted_iota(jnp.int32, (capacity, tokens), 0) == slots[k : k + 1, :]


def as_bf16(mask):
    return jnp.where(mask, 1.0, 0.0).astype(BF16)


def start_columns(source, target, sems):
    copies = []
    for at in range(0, target.shape[1], CHUNK):
        cols = pl.ds(at, CHUNK)
        copies.append(
            pltpu.make_async_copy(source.at[:, cols], target.at[:, cols], sems.at[at // CHUNK])
        )
        copies[-1].start()
    return copies


def dispatch_grads(count, ids_ref, gates_ref, grad_hbm, *refs):
    out_refs = refs[:count]
    slots_ref, table_ref, grad_ref, sems = refs[count:]
    width = grad_ref.shape[1]
    copies = start_columns(grad_hbm, grad_ref, sems)
    slots, first = slots_from(ids_ref[...])
    slots_ref[...] = slots
    gates = jnp.where(first, gates_ref[0:1, :], gates_ref[1:2, :])
    table_ref[...] = gates
    masks = [one_hot(slots, k, out_refs[k].shape[0]) for k in range(count)]
    picks = [as_bf16(mask) for mask in masks]
    scales = [
        jnp.sum(jnp.where(masks[k], gates[k : k + 1, :], 0.0), axis=1, keepdims=True)
        for k in range(count)
    ]
    for at in range(0, width, CHUNK):
        cols = slice(at, at + CHUNK)
        copies[at // CHUNK].wait()
        for k in range(count):
            rows = jnp.dot(picks[k], grad_ref[:, cols], preferred_element_type=F32)
            out_refs[k][:, cols] = (rows * scales[k]).astype(BF16)


def attend(parts, hops, slots_ref, *refs):
    query_hbm, residual_hbm, gain_hbm, own_hbm = refs[0:4]
    other_refs = refs[4 : 3 + parts]
    stream_ref, left_ref, right_ref = refs[3 + parts : 6 + parts]
    query_ref, residual_ref, gain_ref, own_ref = refs[6 + parts : 10 + parts]
    query_sems, residual_sems, gain_sem, own_sem = refs[10 + parts :]
    tokens, width = query_ref.shape
    own_copy = pltpu.make_async_copy(own_hbm, own_ref, own_sem)
    own_copy.start()
    query_copies = start_columns(query_hbm, query_ref, query_sems)
    residual_copies = start_columns(residual_hbm, residual_ref, residual_sems)
    gain_copy = pltpu.make_async_copy(gain_hbm, gain_ref, gain_sem)
    gain_copy.start()
    memory_refs = (own_ref,) + tuple(other_refs)
    heads = GROUP // HEAD_SIZE
    rows = sum(ref.shape[1] for ref in memory_refs)
    own = (
        lax.broadcasted_iota(jnp.int32, (heads * rows, GROUP), 0) // rows
        == lax.broadcasted_iota(jnp.int32, (heads * rows, GROUP), 1) // HEAD_SIZE
    )
    total = jnp.zeros((tokens, 1), F32)

    def spread(which, cols):
        piece = jnp.concatenate([ref[which, :, cols] for ref in memory_refs], axis=0)
        return jnp.where(own, jnp.concatenate([piece] * heads, axis=0), jnp.zeros((), BF16))

    own_copy.wait()
    for at in range(0, width, GROUP):
        cols = slice(at, at + GROUP)
        if at % CHUNK == 0:
            query_copies[at // CHUNK].wait()
            residual_copies[at // CHUNK].wait()
        scores = lax.dot_general(
            spread(0, cols), query_ref[:, cols], (((1,), (1,)), ((), ())), preferred_element_type=F32
        ) * HEAD_SIZE ** (-0.5)
        scores = scores.reshape(heads, rows, tokens)
        exponent = jnp.exp(scores - jnp.max(scores, axis=1, keepdims=True))
        probs = exponent / jnp.sum(exponent, axis=1, keepdims=True)
        attended = lax.dot_general(
            probs.reshape(heads * rows, tokens).astype(BF16),
            spread(1, cols),
            (((0,), (0,)), ((), ())),
            preferred_element_type=F32,
        ).astype(BF16)
        stream = residual_ref[:, cols].astype(F32) + attended.astype(F32)
        stream_ref[:, cols] = stream
        total = total + jnp.sum(stream * stream, axis=1, keepdims=True)
    gain_copy.wait()
    scale = lax.rsqrt(total / width + 1e-06)
    half = width // 2
    for at in range(0, width, GROUP):
        cols = slice(at, at + GROUP)
        gain = gain_ref[cols].reshape(1, GROUP)
        piece = (stream_ref[:, cols] * scale * gain).astype(BF16)
        if at < half:
            left_ref[0:tokens, cols] = piece
        else:
            right_ref[0:tokens, at - half : at - half + GROUP] = piece
    if hops:
        slots = slots_ref[...]
        relay(right_ref, slots, None, 1, left_ref, slice(tokens, None))
        relay(left_ref, slots, None, 2, right_ref, slice(tokens, None))


def slots_from(ids):
    tokens = ids.shape[1]
    me = lax.axis_index("expert")
    expert = lax.broadcasted_iota(jnp.int32, (8, tokens), 0) ^ me
    first = ids[0:1, :] == expert
    chosen = first | (ids[1:2, :] == expert)
    earlier = lax.broadcasted_iota(jnp.int32, (tokens, tokens), 0) < lax.broadcasted_iota(
        jnp.int32, (tokens, tokens), 1
    )
    count = jnp.dot(as_bf16(chosen), as_bf16(earlier), preferred_element_type=F32)
    return jnp.where(chosen, count.astype(jnp.int32), -1), first


def split_grads(ids_hbm, gates_hbm, grad_hbm, left_ref, right_ref, slots_ref, table_ref, *scratch):
    ids_ref, gates_ref, sems = scratch
    tokens, half = grad_hbm.shape[0], left_ref.shape[1]
    copies = [
        pltpu.make_async_copy(ids_hbm, ids_ref, sems.at[0]),
        pltpu.make_async_copy(gates_hbm, gates_ref, sems.at[1]),
    ]
    for side, target in enumerate((left_ref, right_ref)):
        for part in range(2):
            rows = pl.ds(part * (tokens // 2), tokens // 2)
            copies.append(
                pltpu.make_async_copy(
                    grad_hbm.at[rows, pl.ds(side * half, half)],
                    target.at[rows, :],
                    sems.at[2 + 2 * side + part],
                )
            )
    for copy in copies:
        copy.start()
    copies[0].wait()
    copies[1].wait()
    gates = gates_ref[...]
    high = gates.astype(BF16).astype(F32)
    middle = (gates - high).astype(BF16).astype(F32)
    low = gates - high - middle
    notes = jnp.concatenate(
        [ids_ref[...].astype(F32), high, middle, low, jnp.zeros((8, tokens), F32)], axis=0
    ).astype(BF16)
    for target in (left_ref, right_ref):
        target[tokens : tokens + 16, :] = jnp.zeros((16, half), BF16)
        target[tokens : tokens + 16, 0:tokens] = notes
    slots, first = slots_from(ids_ref[...])
    table = jnp.where(first, gates[0:1, :], gates[1:2, :])
    slots_ref[...], table_ref[...] = slots, table
    for copy in copies[2:]:
        copy.wait()
    relay(right_ref, slots, table, 1, left_ref, slice(tokens + 16, None))
    relay(left_ref, slots, table, 2, right_ref, slice(tokens + 16, None))


def notes_of(ref, tokens):
    notes = ref[tokens : tokens + 16, 0:tokens].astype(F32)
    slots, first = slots_from(notes[0:2].astype(jnp.int32))
    gates = notes[2:4] + notes[4:6] + notes[6:8]
    return slots, jnp.where(first, gates[0:1, :], gates[1:2, :])


def relay(ref, slots, gates, k, out_ref, place, shift=0):
    tokens = slots.shape[1]
    rows_at = range(*place.indices(out_ref.shape[0]))
    mask = one_hot(slots, k, len(rows_at))
    pick = as_bf16(mask)
    if gates is not None:
        gate = jnp.sum(jnp.where(mask, gates[k : k + 1, :], 0.0), axis=1, keepdims=True)
    for at in range(0, ref.shape[1], GROUP):
        rows = jnp.dot(pick, ref[0:tokens, at : at + GROUP], preferred_element_type=F32)
        if gates is not None:
            rows = rows * gate
        out_ref[place, shift + at : shift + at + GROUP] = rows.astype(BF16)


def gather_near(own, by_x, by_y, blocks, direct, near_ref):
    (own_slots, own_gates), (x_slots, x_gates), (y_slots, y_gates) = own, by_x, by_y
    left_ref, right_ref, x_ref, y_ref = blocks
    capacity, half = near_ref.shape[0] // 3, left_ref.shape[1]
    here, at_x, at_y = (slice(k * capacity, (k + 1) * capacity) for k in range(3))
    relay(left_ref, own_slots, own_gates, 0, near_ref, here)
    relay(right_ref, own_slots, own_gates, 0, near_ref, here, half)
    relay(x_ref, x_slots, x_gates, 0, near_ref, at_x)
    near_ref[at_x, half:] = x_ref[direct, :]
    near_ref[at_y, 0:half] = y_ref[direct, :]
    relay(y_ref, y_slots, y_gates, 0, near_ref, at_y, half)


def relay_grads(left_ref, right_ref, x_ref, y_ref, slots_ref, table_ref, *refs):
    pass_left, pass_right, near_ref, others_ref = refs
    tokens = slots_ref.shape[1]
    x_notes, y_notes = notes_of(x_ref, tokens), notes_of(y_ref, tokens)
    others_ref[0:8, :], others_ref[8:16, :] = x_notes[0], y_notes[0]
    relay(x_ref, *x_notes, 2, pass_left, slice(None))
    relay(y_ref, *y_notes, 1, pass_right, slice(None))
    blocks = (left_ref, right_ref, x_ref, y_ref)
    own = (slots_ref[...], table_ref[...])
    gather_near(own, x_notes, y_notes, blocks, slice(tokens + 16, None), near_ref)


def relay_rows(left_ref, right_ref, x_ref, y_ref, slots_ref, others_ref, *refs):
    pass_left, pass_right, near_ref = refs
    by_x, by_y = (others_ref[0:8, :], None), (others_ref[8:16, :], None)
    relay(x_ref, *by_x, 2, pass_left, slice(None))
    relay(y_ref, *by_y, 1, pass_right, slice(None))
    blocks = (left_ref, right_ref, x_ref, y_ref)
    direct = slice(slots_ref.shape[1], None)
    gather_near((slots_ref[...], None), by_x, by_y, blocks, direct, near_ref)


def activate(value):
    square = value * value
    curve = jnp.tanh(GELU_C * (value + GELU_A * square * value))
    hidden = (0.5 * value * (1.0 + curve)).astype(BF16)
    slope = 0.5 * (1.0 + curve) + 0.5 * value * (1.0 - curve * curve) * (
        GELU_C * (1.0 + 3.0 * GELU_A * square)
    )
    return hidden, slope


def back_near(near_ref, out_ref, back_ref):
    back_ref[...] = hidden_grad(near_ref, out_ref)


def experts_near(near_ref, back_ref, in_ref, out_ref, *refs):
    result_refs, grad_ref = refs[0:3], refs[3]
    hidden, slope = activate(hidden_grad(near_ref, in_ref))
    grad_ref[...] = (back_ref[...] * slope).astype(BF16)
    size = result_refs[0].shape[0]
    for at in range(0, out_ref.shape[1], CHUNK):
        cols = slice(at, at + CHUNK)
        rows = jnp.dot(hidden, out_ref[:, cols], preferred_element_type=F32).astype(BF16)
        for k in range(3):
            result_refs[k][:, cols] = rows[k * size : (k + 1) * size]


def weight_grads_near(near_ref, grad_ref, total_ref):
    total_ref[...] = lax.dot_general(
        near_ref[...], grad_ref[...], (((0,), (0,)), ((), ())), preferred_element_type=F32
    )


def finish_far(shards, *refs):
    left_ref, right_ref, grad_left, grad_right, in_ref, out_ref, total_ref = refs[0:7]
    hidden_ref, keep_ref, send_ref = refs[7:]
    half = left_ref.shape[1]

    def narrow(left, right, matrix_ref):
        return sum(
            lax.dot_general(
                ref[...], matrix_ref[:, at : at + half], (((1,), (1,)), ((), ())),
                preferred_element_type=F32,
            )
            for ref, at in ((left, 0), (right, half))
        )

    hidden, slope = activate(narrow(left_ref, right_ref, in_ref))
    hidden_ref[...] = hidden
    grads = (narrow(grad_left, grad_right, out_ref) * slope).astype(BF16)
    halves = [
        lax.dot_general(ref[...], grads, (((0,), (0,)), ((), ())), preferred_element_type=F32)
        for ref in (left_ref, right_ref)
    ]
    block = total_ref.shape[0] // (2 * shards)
    core = lax.axis_index("seq")
    for shard in range(shards):
        full = halves[2 * shard // shards]
        at, there = (2 * shard) % shards * block, 2 * shard * block
        even = pack(full[at : at + block] + total_ref[there : there + block, :])
        odd = pack(
            full[at + block : at + 2 * block] + total_ref[there + block : there + 2 * block, :]
        )
        keep_ref[shard] = jnp.where(core == 0, even, odd)
        send_ref[shard] = jnp.where(core == 0, odd, even).astype(BF16)


def widen(hidden_ref, out_ref, result_ref):
    for at in range(0, out_ref.shape[1], CHUNK):
        cols = slice(at, at + CHUNK)
        result_ref[:, cols] = jnp.dot(
            hidden_ref[...], out_ref[:, cols], preferred_element_type=F32
        ).astype(BF16)


def dispatch_rows(count, slots_ref, left_ref, right_ref, *out_refs):
    half = left_ref.shape[1]
    slots = slots_ref[...]
    for k in range(count):
        pick = as_bf16(one_hot(slots, k, out_refs[k].shape[0]))
        for at in range(0, half, GROUP):
            cols = slice(at, at + GROUP)
            there = slice(half + at, half + at + GROUP)
            out_refs[k][:, cols] = jnp.dot(
                pick, left_ref[:, cols], preferred_element_type=F32
            ).astype(BF16)
            out_refs[k][:, there] = jnp.dot(
                pick, right_ref[:, cols], preferred_element_type=F32
            ).astype(BF16)


def forward(rows_ref, in_ref, out_ref, result_ref):
    hidden, slope = activate(
        lax.dot_general(
            rows_ref[...], in_ref[...], (((1,), (1,)), ((), ())), preferred_element_type=F32
        )
    )
    for at in range(0, out_ref.shape[1], CHUNK):
        cols = slice(at, at + CHUNK)
        result_ref[:, cols] = jnp.dot(
            hidden, out_ref[:, cols], preferred_element_type=F32
        ).astype(BF16)
    return slope


def hidden_grad(grad_ref, out_ref):
    return lax.dot_general(
        grad_ref[...], out_ref[...], (((1,), (1,)), ((), ())), preferred_element_type=F32
    )


def expert_first(count, *refs):
    rows_refs, grad_refs = refs[0:count], refs[count : 2 * count + 1]
    in_ref, out_ref = refs[2 * count + 1 : 2 * count + 3]
    result_refs = refs[2 * count + 3 : 3 * count + 3]
    back_refs, last_ref = refs[3 * count + 3 : 4 * count + 3], refs[4 * count + 3]
    for k in range(count):
        slope = forward(rows_refs[k], in_ref, out_ref, result_refs[k])
        back_refs[k][...] = (hidden_grad(grad_refs[k], out_ref) * slope).astype(BF16)
    last_ref[...] = hidden_grad(grad_refs[count], out_ref)


def expert_last(rows_ref, back_ref, in_ref, out_ref, result_ref, grad_ref):
    slope = forward(rows_ref, in_ref, out_ref, result_ref)
    grad_ref[...] = (back_ref[...] * slope).astype(BF16)


def sum_of_products(rows_refs, grad_refs):
    rows = jnp.concatenate([ref[...] for ref in rows_refs], axis=0)
    grads = jnp.concatenate([ref[...] for ref in grad_refs], axis=0)
    return lax.dot_general(rows, grads, (((0,), (0,)), ((), ())), preferred_element_type=F32)


def pack(block):
    rows, columns = block.shape
    full = columns // 128 * 128
    pieces = [block[:, at : at + 128] for at in range(0, full, 128)]
    pieces.append(
        jnp.concatenate([block[: rows // 2, full:], block[rows // 2 :, full:]], axis=1)
    )
    return jnp.concatenate(pieces, axis=0)


def unpack(packed, rows, columns):
    full = columns // 128 * 128
    last = packed[full // 128 * rows :, :]
    half = columns - full
    pieces = [packed[at * rows : (at + 1) * rows, :] for at in range(full // 128)]
    pieces.append(jnp.concatenate([last[:, :half], last[:, half:]], axis=0))
    return jnp.concatenate(pieces, axis=1)


def weight_grads_whole(count, *refs):
    refs[2 * count][...] = sum_of_products(refs[0:count], refs[count : 2 * count])


def add_cores(shards, keep_ref, other_ref, own_ref, *send_refs):
    me = lax.axis_index("dp")
    own_ref[...] = keep_ref[me] + other_ref[me].astype(F32)
    for k in range(1, shards):
        send_refs[k - 1][...] = (keep_ref[me ^ k] + other_ref[me ^ k].astype(F32)).astype(BF16)


def add_replicas(own_ref, *refs):
    total = own_ref[...]
    for ref in refs[:-1]:
        total = total + ref[...].astype(F32)
    _, rows, columns = refs[-1].shape
    refs[-1][0] = unpack(total, rows, columns)


def combine(count, slots_ref, gates_ref, stream_ref, *refs):
    back_refs, out_ref = refs[0:count], refs[count]
    slots = slots_ref[...]
    gates = gates_ref[...].T
    width = stream_ref.shape[1]
    picks = [as_bf16(one_hot(slots, k, back_refs[k].shape[0])) for k in range(count)]
    for at in range(0, width, CHUNK):
        cols = slice(at, at + CHUNK)
        total = stream_ref[:, cols]
        for k in range(count):
            row = lax.dot_general(
                picks[k], back_refs[k][:, cols], (((0,), (0,)), ((), ())), preferred_element_type=F32
            )
            total = total + row * gates[:, k : k + 1]
        out_ref[:, cols] = total.astype(BF16)


def swap(value, axis, k):
    return lax.ppermute(value, axis, [(i, i ^ k) for i in range(lax.axis_size(axis))])


def per_device(
    queries, memory, residual, norm_gain, expert_ids, route_gates, weight_in, weight_out, layer_grad
):
    tokens, width = queries.shape
    hidden_width = weight_in.shape[2]
    experts, replicas, cores = (lax.axis_size(axis) for axis in ("expert", "dp", "seq"))
    capacity = (5 * tokens + 2 * experts - 1) // (2 * experts)
    capacity = (capacity + 15) // 16 * 16
    half = width // 2
    in_hbm = functools.partial(pltpu.with_memory_space_constraint, memory_space=pltpu.HBM)
    ids, gates = in_hbm(expert_ids.T), in_hbm(route_gates.T)
    layer_grad, queries, residual = in_hbm(layer_grad), in_hbm(queries), in_hbm(residual)
    matrix_in, matrix_out = weight_in[0].T, weight_out[0]
    table = shape((8, tokens), F32)
    vmem, hbm = pltpu.VMEM, pltpu.HBM

    if cores == 2:
        memories = [swap(memory, "seq", 1)]
        own_memory = in_hbm(memory)
    else:
        memories = []
        own_memory = in_hbm(lax.all_gather(memory, "seq", axis=1, tiled=True))
    parts = 1 + len(memories)
    dma = pltpu.SemaphoreType.DMA
    block = width // (replicas * cores)
    hops = experts == 4 and cores == 2 and replicas == 4 and block % 32 == 0
    hops = hops and hidden_width % 128 == 64
    extra = capacity if hops else 0
    attend_call = call(
        functools.partial(attend, parts, hops),
        [shape((tokens, width), F32)] + [shape((tokens + extra, half), BF16)] * 2,
        [vmem((tokens, width), BF16)] * 2
        + [vmem((width,), F32), vmem(own_memory.shape, BF16)]
        + [dma((width // CHUNK,))] * 2
        + [dma, dma],
        [vmem] + [hbm] * 4 + [vmem] * len(memories),
    )
    attend_inputs = (queries, residual, in_hbm(norm_gain), own_memory, *memories)
    integers = shape((8, tokens), jnp.int32)

    if hops:
        first_hop = shape((tokens + 16 + capacity, half), BF16)
        second_hop = shape((capacity, half), BF16)
        near = shape((3 * capacity, width), BF16)
        near_narrow = (3 * capacity, hidden_width)
        left, right, slots, gates = call(
            split_grads,
            [first_hop] * 2 + [integers, table],
            [vmem((2, tokens), jnp.int32), vmem((2, tokens), F32), dma((6,))],
            [hbm] * 3,
        )(ids, gates, layer_grad)
        by_x, by_y = swap(left, "expert", 1), swap(right, "expert", 2)
        stream, left_rows, right_rows = attend_call(slots, *attend_inputs)
        rows_x, rows_y = swap(left_rows, "expert", 1), swap(right_rows, "expert", 2)
        pass_left, pass_right, near_grads, others = call(
            relay_grads, [second_hop] * 2 + [near, shape((16, tokens), jnp.int32)]
        )(left, right, by_x, by_y, slots, gates)
        far_grads = (swap(pass_left, "expert", 2), swap(pass_right, "expert", 1))
        pass_left, pass_right, near_rows = call(relay_rows, [second_hop] * 2 + [near])(
            left_rows, right_rows, rows_x, rows_y, slots, others
        )
        far_rows = (swap(pass_left, "expert", 2), swap(pass_right, "expert", 1))
        back = call(back_near, shape(near_narrow, F32))(near_grads, matrix_out)
        result_shape = shape((capacity, width), BF16)
        *results, near_pre = call(experts_near, [result_shape] * 3 + [shape(near_narrow, BF16)])(
            near_rows, back, matrix_in, matrix_out
        )
        total = call(weight_grads_near, shape((width, hidden_width), F32))(near_rows, near_pre)
        packed = (replicas, block * hidden_width // 128, 128)
        hidden, keep, send = call(
            functools.partial(finish_far, replicas),
            [shape((capacity, hidden_width), BF16), shape(packed, F32), shape(packed, BF16)],
        )(*far_rows, *far_grads, matrix_in, matrix_out, total)
        results.append(call(widen, result_shape)(hidden, matrix_out))
        own, *sends = call(
            functools.partial(add_cores, replicas),
            [shape(packed[1:], F32)] + [shape(packed[1:], BF16)] * (replicas - 1),
        )(keep, swap(send, "seq", 1))
        received = [swap(sends[k - 1], "dp", k) for k in range(1, replicas)]
        grads_here = call(add_replicas, shape((1, block, hidden_width), F32))(own, *received)
    else:
        rows_shape = [shape((capacity, width), BF16)] * experts
        *grads, slots, gates = call(
            functools.partial(dispatch_grads, experts),
            rows_shape + [integers, table],
            [vmem((tokens, width), BF16), dma((width // CHUNK,))],
            [vmem, vmem, hbm],
        )(expert_ids.T, route_gates.T, layer_grad)
        grads = [grads[0]] + [swap(grads[k], "expert", k) for k in range(1, experts)]
        stream, left, right = attend_call(slots, *attend_inputs)
        rows = call(functools.partial(dispatch_rows, experts), rows_shape)(slots, left, right)
        rows = [rows[0]] + [swap(rows[k], "expert", k) for k in range(1, experts)]
        last = experts - 1
        back_shape = shape((capacity, hidden_width), BF16)
        outs = call(
            functools.partial(expert_first, last),
            rows_shape[:last] + [back_shape] * last + [shape((capacity, hidden_width), F32)],
        )(*rows[:last], *grads, matrix_in, matrix_out)
        result, back = call(expert_last, [rows_shape[0], back_shape])(
            rows[last], outs[2 * last], matrix_in, matrix_out
        )
        results = list(outs[:last]) + [result]
        whole = call(
            functools.partial(weight_grads_whole, experts), shape((width, hidden_width), F32)
        )(*rows, *outs[last : 2 * last], back)
        grads_here = lax.psum_scatter(whole, ("dp", "seq"), scatter_dimension=0, tiled=True)[None]
    results = [results[0]] + [swap(results[k], "expert", k) for k in range(1, experts)]

    layer_output = call(functools.partial(combine, experts), shape((tokens, width), BF16))(
        slots, gates, stream, *results
    )
    return layer_output, grads_here


def solution(mesh):
    rows = P(("dp", "expert", "seq"), None)
    return jax.shard_map(
        per_device,
        mesh=mesh,
        in_specs=(
            rows,
            P(None, ("dp", "expert", "seq"), None),
            rows,
            P(),
            rows,
            rows,
            P("expert", None, None),
            P("expert", None, None),
            rows,
        ),
        out_specs=(rows, P("expert", ("dp", "seq"), None)),
        check_vma=False,
    )
```

```python
import functools

import jax
import jax.numpy as jnp
from jax import lax
from jax.experimental import pallas as pl
from jax.experimental.pallas import tpu as pltpu
from jax.sharding import PartitionSpec as P

HEAD_SIZE = 64
GROUP = 256
CHUNK = 512
VMEM_LIMIT = 24 * 1024 * 1024
GELU_C = 0.7978845608028654
GELU_A = 0.044715
BF16 = jnp.bfloat16
F32 = jnp.float32


def params():
    return pltpu.CompilerParams(vmem_limit_bytes=VMEM_LIMIT)


def call(kernel, out_shapes, scratch=(), inputs=None):
    specs = {} if inputs is None else {"in_specs": [pl.BlockSpec(memory_space=at) for at in inputs]}
    return pl.pallas_call(
        kernel,
        out_shape=out_shapes,
        scratch_shapes=list(scratch),
        compiler_params=params(),
        **specs,
    )


def shape(dims, dtype):
    return jax.ShapeDtypeStruct(dims, dtype)


def one_hot(slots, k, capacity):
    tokens = slots.shape[1]
    return lax.broadcasted_iota(jnp.int32, (capacity, tokens), 0) == slots[k : k + 1, :]


def as_bf16(mask):
    return jnp.where(mask, 1.0, 0.0).astype(BF16)


def start_columns(source, target, sems):
    copies = []
    for at in range(0, target.shape[1], CHUNK):
        cols = pl.ds(at, CHUNK)
        copies.append(
            pltpu.make_async_copy(source.at[:, cols], target.at[:, cols], sems.at[at // CHUNK])
        )
        copies[-1].start()
    return copies


def dispatch_grads(count, ids_ref, gates_ref, grad_hbm, *refs):
    out_refs = refs[:count]
    slots_ref, table_ref, grad_ref, sems = refs[count:]
    width = grad_ref.shape[1]
    copies = start_columns(grad_hbm, grad_ref, sems)
    slots, first = slots_from(ids_ref[...])
    slots_ref[...] = slots
    gates = jnp.where(first, gates_ref[0:1, :], gates_ref[1:2, :])
    table_ref[...] = gates
    masks = [one_hot(slots, k, out_refs[k].shape[0]) for k in range(count)]
    picks = [as_bf16(mask) for mask in masks]
    scales = [
        jnp.sum(jnp.where(masks[k], gates[k : k + 1, :], 0.0), axis=1, keepdims=True)
        for k in range(count)
    ]
    for at in range(0, width, CHUNK):
        cols = slice(at, at + CHUNK)
        copies[at // CHUNK].wait()
        for k in range(count):
            rows = jnp.dot(picks[k], grad_ref[:, cols], preferred_element_type=F32)
            out_refs[k][:, cols] = (rows * scales[k]).astype(BF16)


def attend(parts, hops, slots_ref, *refs):
    query_hbm, residual_hbm, gain_hbm, own_hbm = refs[0:4]
    other_refs = refs[4 : 3 + parts]
    stream_ref, left_ref, right_ref = refs[3 + parts : 6 + parts]
    query_ref, residual_ref, gain_ref, own_ref = refs[6 + parts : 10 + parts]
    query_sems, residual_sems, gain_sem, own_sem = refs[10 + parts :]
    tokens, width = query_ref.shape
    own_copy = pltpu.make_async_copy(own_hbm, own_ref, own_sem)
    own_copy.start()
    query_copies = start_columns(query_hbm, query_ref, query_sems)
    residual_copies = start_columns(residual_hbm, residual_ref, residual_sems)
    gain_copy = pltpu.make_async_copy(gain_hbm, gain_ref, gain_sem)
    gain_copy.start()
    memory_refs = (own_ref,) + tuple(other_refs)
    heads = GROUP // HEAD_SIZE
    rows = sum(ref.shape[1] for ref in memory_refs)
    own = (
        lax.broadcasted_iota(jnp.int32, (heads * rows, GROUP), 0) // rows
        == lax.broadcasted_iota(jnp.int32, (heads * rows, GROUP), 1) // HEAD_SIZE
    )
    total = jnp.zeros((tokens, 1), F32)

    def spread(which, cols):
        piece = jnp.concatenate([ref[which, :, cols] for ref in memory_refs], axis=0)
        return jnp.where(own, jnp.concatenate([piece] * heads, axis=0), jnp.zeros((), BF16))

    own_copy.wait()
    for at in range(0, width, GROUP):
        cols = slice(at, at + GROUP)
        if at % CHUNK == 0:
            query_copies[at // CHUNK].wait()
            residual_copies[at // CHUNK].wait()
        scores = lax.dot_general(
            spread(0, cols), query_ref[:, cols], (((1,), (1,)), ((), ())), preferred_element_type=F32
        ) * HEAD_SIZE ** (-0.5)
        scores = scores.reshape(heads, rows, tokens)
        exponent = jnp.exp(scores - jnp.max(scores, axis=1, keepdims=True))
        probs = exponent / jnp.sum(exponent, axis=1, keepdims=True)
        attended = lax.dot_general(
            probs.reshape(heads * rows, tokens).astype(BF16),
            spread(1, cols),
            (((0,), (0,)), ((), ())),
            preferred_element_type=F32,
        ).astype(BF16)
        stream = residual_ref[:, cols].astype(F32) + attended.astype(F32)
        stream_ref[:, cols] = stream
        total = total + jnp.sum(stream * stream, axis=1, keepdims=True)
    gain_copy.wait()
    scale = lax.rsqrt(total / width + 1e-06)
    half = width // 2
    for at in range(0, width, GROUP):
        cols = slice(at, at + GROUP)
        gain = gain_ref[cols].reshape(1, GROUP)
        piece = (stream_ref[:, cols] * scale * gain).astype(BF16)
        if at < half:
            left_ref[0:tokens, cols] = piece
        else:
            right_ref[0:tokens, at - half : at - half + GROUP] = piece
    if hops:
        slots = slots_ref[...]
        relay(right_ref, slots, None, 1, left_ref, slice(tokens, None))
        relay(left_ref, slots, None, 2, right_ref, slice(tokens, None))


def slots_from(ids):
    tokens = ids.shape[1]
    me = lax.axis_index("expert")
    expert = lax.broadcasted_iota(jnp.int32, (8, tokens), 0) ^ me
    first = ids[0:1, :] == expert
    chosen = first | (ids[1:2, :] == expert)
    earlier = lax.broadcasted_iota(jnp.int32, (tokens, tokens), 0) < lax.broadcasted_iota(
        jnp.int32, (tokens, tokens), 1
    )
    count = jnp.dot(as_bf16(chosen), as_bf16(earlier), preferred_element_type=F32)
    return jnp.where(chosen, count.astype(jnp.int32), -1), first


def split_grads(ids_hbm, gates_hbm, grad_hbm, left_ref, right_ref, slots_ref, table_ref, *scratch):
    ids_ref, gates_ref, sems = scratch
    tokens, half = grad_hbm.shape[0], left_ref.shape[1]
    copies = [
        pltpu.make_async_copy(ids_hbm, ids_ref, sems.at[0]),
        pltpu.make_async_copy(gates_hbm, gates_ref, sems.at[1]),
    ]
    for side, target in enumerate((left_ref, right_ref)):
        for part in range(2):
            rows = pl.ds(part * (tokens // 2), tokens // 2)
            copies.append(
                pltpu.make_async_copy(
                    grad_hbm.at[rows, pl.ds(side * half, half)],
                    target.at[rows, :],
                    sems.at[2 + 2 * side + part],
                )
            )
    for copy in copies:
        copy.start()
    copies[0].wait()
    copies[1].wait()
    gates = gates_ref[...]
    high = gates.astype(BF16).astype(F32)
    middle = (gates - high).astype(BF16).astype(F32)
    low = gates - high - middle
    notes = jnp.concatenate(
        [ids_ref[...].astype(F32), high, middle, low, jnp.zeros((8, tokens), F32)], axis=0
    ).astype(BF16)
    for target in (left_ref, right_ref):
        target[tokens : tokens + 16, :] = jnp.zeros((16, half), BF16)
        target[tokens : tokens + 16, 0:tokens] = notes
    slots, first = slots_from(ids_ref[...])
    table = jnp.where(first, gates[0:1, :], gates[1:2, :])
    slots_ref[...], table_ref[...] = slots, table
    for copy in copies[2:]:
        copy.wait()
    relay(right_ref, slots, table, 1, left_ref, slice(tokens + 16, None))
    relay(left_ref, slots, table, 2, right_ref, slice(tokens + 16, None))


def notes_of(ref, tokens):
    notes = ref[tokens : tokens + 16, 0:tokens].astype(F32)
    slots, first = slots_from(notes[0:2].astype(jnp.int32))
    gates = notes[2:4] + notes[4:6] + notes[6:8]
    return slots, jnp.where(first, gates[0:1, :], gates[1:2, :])


def relay(ref, slots, gates, k, out_ref, place, shift=0):
    tokens = slots.shape[1]
    rows_at = range(*place.indices(out_ref.shape[0]))
    mask = one_hot(slots, k, len(rows_at))
    pick = as_bf16(mask)
    if gates is not None:
        gate = jnp.sum(jnp.where(mask, gates[k : k + 1, :], 0.0), axis=1, keepdims=True)
    for at in range(0, ref.shape[1], GROUP):
        rows = jnp.dot(pick, ref[0:tokens, at : at + GROUP], preferred_element_type=F32)
        if gates is not None:
            rows = rows * gate
        out_ref[place, shift + at : shift + at + GROUP] = rows.astype(BF16)


def gather_near(own, by_x, by_y, blocks, direct, near_ref):
    (own_slots, own_gates), (x_slots, x_gates), (y_slots, y_gates) = own, by_x, by_y
    left_ref, right_ref, x_ref, y_ref = blocks
    capacity, half = near_ref.shape[0] // 3, left_ref.shape[1]
    here, at_x, at_y = (slice(k * capacity, (k + 1) * capacity) for k in range(3))
    relay(left_ref, own_slots, own_gates, 0, near_ref, here)
    relay(right_ref, own_slots, own_gates, 0, near_ref, here, half)
    relay(x_ref, x_slots, x_gates, 0, near_ref, at_x)
    near_ref[at_x, half:] = x_ref[direct, :]
    near_ref[at_y, 0:half] = y_ref[direct, :]
    relay(y_ref, y_slots, y_gates, 0, near_ref, at_y, half)


def relay_grads(left_ref, right_ref, x_ref, y_ref, slots_ref, table_ref, *refs):
    pass_left, pass_right, near_ref, others_ref = refs
    tokens = slots_ref.shape[1]
    x_notes, y_notes = notes_of(x_ref, tokens), notes_of(y_ref, tokens)
    others_ref[0:8, :], others_ref[8:16, :] = x_notes[0], y_notes[0]
    relay(x_ref, *x_notes, 2, pass_left, slice(None))
    relay(y_ref, *y_notes, 1, pass_right, slice(None))
    blocks = (left_ref, right_ref, x_ref, y_ref)
    own = (slots_ref[...], table_ref[...])
    gather_near(own, x_notes, y_notes, blocks, slice(tokens + 16, None), near_ref)


def relay_rows(left_ref, right_ref, x_ref, y_ref, slots_ref, others_ref, *refs):
    pass_left, pass_right, near_ref = refs
    by_x, by_y = (others_ref[0:8, :], None), (others_ref[8:16, :], None)
    relay(x_ref, *by_x, 2, pass_left, slice(None))
    relay(y_ref, *by_y, 1, pass_right, slice(None))
    blocks = (left_ref, right_ref, x_ref, y_ref)
    direct = slice(slots_ref.shape[1], None)
    gather_near((slots_ref[...], None), by_x, by_y, blocks, direct, near_ref)


def activate(value):
    square = value * value
    curve = jnp.tanh(GELU_C * (value + GELU_A * square * value))
    hidden = (0.5 * value * (1.0 + curve)).astype(BF16)
    slope = 0.5 * (1.0 + curve) + 0.5 * value * (1.0 - curve * curve) * (
        GELU_C * (1.0 + 3.0 * GELU_A * square)
    )
    return hidden, slope


def back_near(near_ref, out_ref, back_ref):
    back_ref[...] = hidden_grad(near_ref, out_ref)


def experts_near(near_ref, back_ref, in_ref, out_ref, *refs):
    result_refs, grad_ref = refs[0:3], refs[3]
    hidden, slope = activate(hidden_grad(near_ref, in_ref))
    grad_ref[...] = (back_ref[...] * slope).astype(BF16)
    size = result_refs[0].shape[0]
    for at in range(0, out_ref.shape[1], CHUNK):
        cols = slice(at, at + CHUNK)
        rows = jnp.dot(hidden, out_ref[:, cols], preferred_element_type=F32).astype(BF16)
        for k in range(3):
            result_refs[k][:, cols] = rows[k * size : (k + 1) * size]


def weight_grads_near(near_ref, grad_ref, total_ref):
    total_ref[...] = lax.dot_general(
        near_ref[...], grad_ref[...], (((0,), (0,)), ((), ())), preferred_element_type=F32
    )


def finish_far(shards, *refs):
    left_ref, right_ref, grad_left, grad_right, in_ref, out_ref, total_ref = refs[0:7]
    hidden_ref, keep_ref, send_ref = refs[7:]
    half = left_ref.shape[1]

    def narrow(left, right, matrix_ref):
        return sum(
            lax.dot_general(
                ref[...], matrix_ref[:, at : at + half], (((1,), (1,)), ((), ())),
                preferred_element_type=F32,
            )
            for ref, at in ((left, 0), (right, half))
        )

    hidden, slope = activate(narrow(left_ref, right_ref, in_ref))
    hidden_ref[...] = hidden
    grads = (narrow(grad_left, grad_right, out_ref) * slope).astype(BF16)
    halves = [
        lax.dot_general(ref[...], grads, (((0,), (0,)), ((), ())), preferred_element_type=F32)
        for ref in (left_ref, right_ref)
    ]
    block = total_ref.shape[0] // (2 * shards)
    core = lax.axis_index("seq")
    for shard in range(shards):
        full = halves[2 * shard // shards]
        at, there = (2 * shard) % shards * block, 2 * shard * block
        even = pack(full[at : at + block] + total_ref[there : there + block, :])
        odd = pack(
            full[at + block : at + 2 * block] + total_ref[there + block : there + 2 * block, :]
        )
        keep_ref[shard] = jnp.where(core == 0, even, odd)
        send_ref[shard] = jnp.where(core == 0, odd, even).astype(BF16)


def widen(hidden_ref, out_ref, result_ref):
    for at in range(0, out_ref.shape[1], CHUNK):
        cols = slice(at, at + CHUNK)
        result_ref[:, cols] = jnp.dot(
            hidden_ref[...], out_ref[:, cols], preferred_element_type=F32
        ).astype(BF16)


def dispatch_rows(count, slots_ref, left_ref, right_ref, *out_refs):
    half = left_ref.shape[1]
    slots = slots_ref[...]
    for k in range(count):
        pick = as_bf16(one_hot(slots, k, out_refs[k].shape[0]))
        for at in range(0, half, GROUP):
            cols = slice(at, at + GROUP)
            there = slice(half + at, half + at + GROUP)
            out_refs[k][:, cols] = jnp.dot(
                pick, left_ref[:, cols], preferred_element_type=F32
            ).astype(BF16)
            out_refs[k][:, there] = jnp.dot(
                pick, right_ref[:, cols], preferred_element_type=F32
            ).astype(BF16)


def forward(rows_ref, in_ref, out_ref, result_ref):
    hidden, slope = activate(
        lax.dot_general(
            rows_ref[...], in_ref[...], (((1,), (1,)), ((), ())), preferred_element_type=F32
        )
    )
    for at in range(0, out_ref.shape[1], CHUNK):
        cols = slice(at, at + CHUNK)
        result_ref[:, cols] = jnp.dot(
            hidden, out_ref[:, cols], preferred_element_type=F32
        ).astype(BF16)
    return slope


def hidden_grad(grad_ref, out_ref):
    return lax.dot_general(
        grad_ref[...], out_ref[...], (((1,), (1,)), ((), ())), preferred_element_type=F32
    )


def expert_first(count, *refs):
    rows_refs, grad_refs = refs[0:count], refs[count : 2 * count + 1]
    in_ref, out_ref = refs[2 * count + 1 : 2 * count + 3]
    result_refs = refs[2 * count + 3 : 3 * count + 3]
    back_refs, last_ref = refs[3 * count + 3 : 4 * count + 3], refs[4 * count + 3]
    for k in range(count):
        slope = forward(rows_refs[k], in_ref, out_ref, result_refs[k])
        back_refs[k][...] = (hidden_grad(grad_refs[k], out_ref) * slope).astype(BF16)
    last_ref[...] = hidden_grad(grad_refs[count], out_ref)


def expert_last(rows_ref, back_ref, in_ref, out_ref, result_ref, grad_ref):
    slope = forward(rows_ref, in_ref, out_ref, result_ref)
    grad_ref[...] = (back_ref[...] * slope).astype(BF16)


def sum_of_products(rows_refs, grad_refs):
    rows = jnp.concatenate([ref[...] for ref in rows_refs], axis=0)
    grads = jnp.concatenate([ref[...] for ref in grad_refs], axis=0)
    return lax.dot_general(rows, grads, (((0,), (0,)), ((), ())), preferred_element_type=F32)


def pack(block):
    rows, columns = block.shape
    full = columns // 128 * 128
    pieces = [block[:, at : at + 128] for at in range(0, full, 128)]
    pieces.append(
        jnp.concatenate([block[: rows // 2, full:], block[rows // 2 :, full:]], axis=1)
    )
    return jnp.concatenate(pieces, axis=0)


def unpack(packed, rows, columns):
    full = columns // 128 * 128
    last = packed[full // 128 * rows :, :]
    half = columns - full
    pieces = [packed[at * rows : (at + 1) * rows, :] for at in range(full // 128)]
    pieces.append(jnp.concatenate([last[:, :half], last[:, half:]], axis=0))
    return jnp.concatenate(pieces, axis=1)


def weight_grads_whole(count, *refs):
    refs[2 * count][...] = sum_of_products(refs[0:count], refs[count : 2 * count])


def add_cores(shards, keep_ref, other_ref, own_ref, *send_refs):
    me = lax.axis_index("dp")
    own_ref[...] = keep_ref[me] + other_ref[me].astype(F32)
    for k in range(1, shards):
        send_refs[k - 1][...] = (keep_ref[me ^ k] + other_ref[me ^ k].astype(F32)).astype(BF16)


def add_replicas(own_ref, *refs):
    total = own_ref[...]
    for ref in refs[:-1]:
        total = total + ref[...].astype(F32)
    _, rows, columns = refs[-1].shape
    refs[-1][0] = unpack(total, rows, columns)


def combine_here(slots_ref, gates_ref, stream_ref, here_ref, total_ref):
    mix_into(slots_ref, gates_ref, 0, stream_ref, (here_ref,), total_ref)


def combine_rest(slots_ref, gates_ref, base_ref, *refs):
    mix_into(slots_ref, gates_ref, 1, base_ref, refs[:-1], refs[-1])


def mix_into(slots_ref, gates_ref, first, base_ref, result_refs, out_ref):
    slots = slots_ref[...]
    gates = gates_ref[...].T
    picks = [
        as_bf16(one_hot(slots, first + k, ref.shape[0])) for k, ref in enumerate(result_refs)
    ]
    for at in range(0, base_ref.shape[1], CHUNK):
        cols = slice(at, at + CHUNK)
        total = base_ref[:, cols]
        for k, ref in enumerate(result_refs):
            row = lax.dot_general(
                picks[k], ref[:, cols], (((0,), (0,)), ((), ())), preferred_element_type=F32
            )
            total = total + row * gates[:, first + k : first + k + 1]
        out_ref[:, cols] = total.astype(out_ref.dtype)


def swap(value, axis, k):
    return lax.ppermute(value, axis, [(i, i ^ k) for i in range(lax.axis_size(axis))])


def per_device(
    queries, memory, residual, norm_gain, expert_ids, route_gates, weight_in, weight_out, layer_grad
):
    tokens, width = queries.shape
    hidden_width = weight_in.shape[2]
    experts, replicas, cores = (lax.axis_size(axis) for axis in ("expert", "dp", "seq"))
    capacity = (5 * tokens + 2 * experts - 1) // (2 * experts)
    capacity = (capacity + 15) // 16 * 16
    half = width // 2
    in_hbm = functools.partial(pltpu.with_memory_space_constraint, memory_space=pltpu.HBM)
    ids, gates = in_hbm(expert_ids.T), in_hbm(route_gates.T)
    layer_grad, queries, residual = in_hbm(layer_grad), in_hbm(queries), in_hbm(residual)
    matrix_in, matrix_out = weight_in[0].T, weight_out[0]
    table = shape((8, tokens), F32)
    vmem, hbm = pltpu.VMEM, pltpu.HBM

    if cores == 2:
        memories = [swap(memory, "seq", 1)]
        own_memory = in_hbm(memory)
    else:
        memories = []
        own_memory = in_hbm(lax.all_gather(memory, "seq", axis=1, tiled=True))
    parts = 1 + len(memories)
    dma = pltpu.SemaphoreType.DMA
    block = width // (replicas * cores)
    hops = experts == 4 and cores == 2 and replicas == 4 and block % 32 == 0
    hops = hops and hidden_width % 128 == 64
    extra = capacity if hops else 0
    attend_call = call(
        functools.partial(attend, parts, hops),
        [shape((tokens, width), F32)] + [shape((tokens + extra, half), BF16)] * 2,
        [vmem((tokens, width), BF16)] * 2
        + [vmem((width,), F32), vmem(own_memory.shape, BF16)]
        + [dma((width // CHUNK,))] * 2
        + [dma, dma],
        [vmem] + [hbm] * 4 + [vmem] * len(memories),
    )
    attend_inputs = (queries, residual, in_hbm(norm_gain), own_memory, *memories)
    integers = shape((8, tokens), jnp.int32)

    if hops:
        first_hop = shape((tokens + 16 + capacity, half), BF16)
        second_hop = shape((capacity, half), BF16)
        near = shape((3 * capacity, width), BF16)
        near_narrow = (3 * capacity, hidden_width)
        left, right, slots, gates = call(
            split_grads,
            [first_hop] * 2 + [integers, table],
            [vmem((2, tokens), jnp.int32), vmem((2, tokens), F32), dma((6,))],
            [hbm] * 3,
        )(ids, gates, layer_grad)
        by_x, by_y = swap(left, "expert", 1), swap(right, "expert", 2)
        stream, left_rows, right_rows = attend_call(slots, *attend_inputs)
        rows_x, rows_y = swap(left_rows, "expert", 1), swap(right_rows, "expert", 2)
        pass_left, pass_right, near_grads, others = call(
            relay_grads, [second_hop] * 2 + [near, shape((16, tokens), jnp.int32)]
        )(left, right, by_x, by_y, slots, gates)
        far_grads = (swap(pass_left, "expert", 2), swap(pass_right, "expert", 1))
        pass_left, pass_right, near_rows = call(relay_rows, [second_hop] * 2 + [near])(
            left_rows, right_rows, rows_x, rows_y, slots, others
        )
        far_rows = (swap(pass_left, "expert", 2), swap(pass_right, "expert", 1))
        back = call(back_near, shape(near_narrow, F32))(near_grads, matrix_out)
        result_shape = shape((capacity, width), BF16)
        *results, near_pre = call(experts_near, [result_shape] * 3 + [shape(near_narrow, BF16)])(
            near_rows, back, matrix_in, matrix_out
        )
        total = call(weight_grads_near, shape((width, hidden_width), F32))(near_rows, near_pre)
        packed = (replicas, block * hidden_width // 128, 128)
        hidden, keep, send = call(
            functools.partial(finish_far, replicas),
            [shape((capacity, hidden_width), BF16), shape(packed, F32), shape(packed, BF16)],
        )(*far_rows, *far_grads, matrix_in, matrix_out, total)
        results.append(call(widen, result_shape)(hidden, matrix_out))
        own, *sends = call(
            functools.partial(add_cores, replicas),
            [shape(packed[1:], F32)] + [shape(packed[1:], BF16)] * (replicas - 1),
        )(keep, swap(send, "seq", 1))
        received = [swap(sends[k - 1], "dp", k) for k in (2, 1, 3)]
        grads_here = call(add_replicas, shape((1, block, hidden_width), F32))(own, *received)
    else:
        rows_shape = [shape((capacity, width), BF16)] * experts
        *grads, slots, gates = call(
            functools.partial(dispatch_grads, experts),
            rows_shape + [integers, table],
            [vmem((tokens, width), BF16), dma((width // CHUNK,))],
            [vmem, vmem, hbm],
        )(expert_ids.T, route_gates.T, layer_grad)
        grads = [grads[0]] + [swap(grads[k], "expert", k) for k in range(1, experts)]
        stream, left, right = attend_call(slots, *attend_inputs)
        rows = call(functools.partial(dispatch_rows, experts), rows_shape)(slots, left, right)
        rows = [rows[0]] + [swap(rows[k], "expert", k) for k in range(1, experts)]
        last = experts - 1
        back_shape = shape((capacity, hidden_width), BF16)
        outs = call(
            functools.partial(expert_first, last),
            rows_shape[:last] + [back_shape] * last + [shape((capacity, hidden_width), F32)],
        )(*rows[:last], *grads, matrix_in, matrix_out)
        result, back = call(expert_last, [rows_shape[0], back_shape])(
            rows[last], outs[2 * last], matrix_in, matrix_out
        )
        results = list(outs[:last]) + [result]
        whole = call(
            functools.partial(weight_grads_whole, experts), shape((width, hidden_width), F32)
        )(*rows, *outs[last : 2 * last], back)
        grads_here = lax.psum_scatter(whole, ("dp", "seq"), scatter_dimension=0, tiled=True)[None]
    results = [results[0]] + [swap(results[k], "expert", k) for k in range(1, experts)]

    base = call(combine_here, shape((tokens, width), F32))(slots, gates, stream, results[0])
    layer_output = call(combine_rest, shape((tokens, width), BF16))(
        slots, gates, base, *results[1:]
    )
    return layer_output, grads_here


def solution(mesh):
    rows = P(("dp", "expert", "seq"), None)
    return jax.shard_map(
        per_device,
        mesh=mesh,
        in_specs=(
            rows,
            P(None, ("dp", "expert", "seq"), None),
            rows,
            P(),
            rows,
            rows,
            P("expert", None, None),
            P("expert", None, None),
            rows,
        ),
        out_specs=(rows, P("expert", ("dp", "seq"), None)),
        check_vma=False,
    )
```

```python
import functools

import jax
import jax.numpy as jnp
from jax import lax
from jax.experimental import pallas as pl
from jax.experimental.pallas import tpu as pltpu
from jax.sharding import PartitionSpec as P

HEAD_SIZE = 64
GROUP = 256
CHUNK = 512
VMEM_LIMIT = 24 * 1024 * 1024
GELU_C = 0.7978845608028654
GELU_A = 0.044715
BF16 = jnp.bfloat16
F32 = jnp.float32


def params():
    return pltpu.CompilerParams(vmem_limit_bytes=VMEM_LIMIT)


def call(kernel, out_shapes, scratch=(), inputs=None):
    specs = {} if inputs is None else {"in_specs": [pl.BlockSpec(memory_space=at) for at in inputs]}
    return pl.pallas_call(
        kernel,
        out_shape=out_shapes,
        scratch_shapes=list(scratch),
        compiler_params=params(),
        **specs,
    )


def shape(dims, dtype):
    return jax.ShapeDtypeStruct(dims, dtype)


def one_hot(slots, k, capacity):
    tokens = slots.shape[1]
    return lax.broadcasted_iota(jnp.int32, (capacity, tokens), 0) == slots[k : k + 1, :]


def as_bf16(mask):
    return jnp.where(mask, 1.0, 0.0).astype(BF16)


def start_columns(source, target, sems):
    copies = []
    for at in range(0, target.shape[1], CHUNK):
        cols = pl.ds(at, CHUNK)
        copies.append(
            pltpu.make_async_copy(source.at[:, cols], target.at[:, cols], sems.at[at // CHUNK])
        )
        copies[-1].start()
    return copies


def dispatch_grads(count, ids_ref, gates_ref, grad_hbm, *refs):
    out_refs = refs[:count]
    slots_ref, table_ref, grad_ref, sems = refs[count:]
    width = grad_ref.shape[1]
    copies = start_columns(grad_hbm, grad_ref, sems)
    slots, first = slots_from(ids_ref[...])
    slots_ref[...] = slots
    gates = jnp.where(first, gates_ref[0:1, :], gates_ref[1:2, :])
    table_ref[...] = gates
    masks = [one_hot(slots, k, out_refs[k].shape[0]) for k in range(count)]
    picks = [as_bf16(mask) for mask in masks]
    scales = [
        jnp.sum(jnp.where(masks[k], gates[k : k + 1, :], 0.0), axis=1, keepdims=True)
        for k in range(count)
    ]
    for at in range(0, width, CHUNK):
        cols = slice(at, at + CHUNK)
        copies[at // CHUNK].wait()
        for k in range(count):
            rows = jnp.dot(picks[k], grad_ref[:, cols], preferred_element_type=F32)
            out_refs[k][:, cols] = (rows * scales[k]).astype(BF16)


def attend(parts, hops, slots_ref, *refs):
    query_hbm, residual_hbm, gain_hbm, own_hbm = refs[0:4]
    other_refs = refs[4 : 3 + parts]
    stream_ref, left_ref, right_ref = refs[3 + parts : 6 + parts]
    query_ref, residual_ref, gain_ref, own_ref = refs[6 + parts : 10 + parts]
    query_sems, residual_sems, gain_sem, own_sem = refs[10 + parts :]
    tokens, width = query_ref.shape
    own_copy = pltpu.make_async_copy(own_hbm, own_ref, own_sem)
    own_copy.start()
    query_copies = start_columns(query_hbm, query_ref, query_sems)
    residual_copies = start_columns(residual_hbm, residual_ref, residual_sems)
    gain_copy = pltpu.make_async_copy(gain_hbm, gain_ref, gain_sem)
    gain_copy.start()
    memory_refs = (own_ref,) + tuple(other_refs)
    heads = GROUP // HEAD_SIZE
    rows = sum(ref.shape[1] for ref in memory_refs)
    own = (
        lax.broadcasted_iota(jnp.int32, (heads * rows, GROUP), 0) // rows
        == lax.broadcasted_iota(jnp.int32, (heads * rows, GROUP), 1) // HEAD_SIZE
    )
    total = jnp.zeros((tokens, 1), F32)

    def spread(which, cols):
        piece = jnp.concatenate([ref[which, :, cols] for ref in memory_refs], axis=0)
        return jnp.where(own, jnp.concatenate([piece] * heads, axis=0), jnp.zeros((), BF16))

    own_copy.wait()
    for at in range(0, width, GROUP):
        cols = slice(at, at + GROUP)
        if at % CHUNK == 0:
            query_copies[at // CHUNK].wait()
            residual_copies[at // CHUNK].wait()
        scores = lax.dot_general(
            spread(0, cols), query_ref[:, cols], (((1,), (1,)), ((), ())), preferred_element_type=F32
        ) * HEAD_SIZE ** (-0.5)
        scores = scores.reshape(heads, rows, tokens)
        exponent = jnp.exp(scores - jnp.max(scores, axis=1, keepdims=True))
        probs = exponent / jnp.sum(exponent, axis=1, keepdims=True)
        attended = lax.dot_general(
            probs.reshape(heads * rows, tokens).astype(BF16),
            spread(1, cols),
            (((0,), (0,)), ((), ())),
            preferred_element_type=F32,
        ).astype(BF16)
        stream = residual_ref[:, cols].astype(F32) + attended.astype(F32)
        stream_ref[:, cols] = stream
        total = total + jnp.sum(stream * stream, axis=1, keepdims=True)
    gain_copy.wait()
    scale = lax.rsqrt(total / width + 1e-06)
    half = width // 2
    for at in range(0, width, GROUP):
        cols = slice(at, at + GROUP)
        gain = gain_ref[cols].reshape(1, GROUP)
        piece = (stream_ref[:, cols] * scale * gain).astype(BF16)
        if at < half:
            left_ref[0:tokens, cols] = piece
        else:
            right_ref[0:tokens, at - half : at - half + GROUP] = piece
    if hops:
        slots = slots_ref[...]
        relay(right_ref, slots, None, 1, left_ref, slice(tokens, None))
        relay(left_ref, slots, None, 2, right_ref, slice(tokens, None))


def slots_from(ids):
    tokens = ids.shape[1]
    me = lax.axis_index("expert")
    expert = lax.broadcasted_iota(jnp.int32, (8, tokens), 0) ^ me
    first = ids[0:1, :] == expert
    chosen = first | (ids[1:2, :] == expert)
    earlier = lax.broadcasted_iota(jnp.int32, (tokens, tokens), 0) < lax.broadcasted_iota(
        jnp.int32, (tokens, tokens), 1
    )
    count = jnp.dot(as_bf16(chosen), as_bf16(earlier), preferred_element_type=F32)
    return jnp.where(chosen, count.astype(jnp.int32), -1), first


def split_grads(ids_hbm, gates_hbm, grad_hbm, left_ref, right_ref, slots_ref, table_ref, *scratch):
    ids_ref, gates_ref, sems = scratch
    tokens, half = grad_hbm.shape[0], left_ref.shape[1]
    copies = [
        pltpu.make_async_copy(ids_hbm, ids_ref, sems.at[0]),
        pltpu.make_async_copy(gates_hbm, gates_ref, sems.at[1]),
    ]
    for side, target in enumerate((left_ref, right_ref)):
        for part in range(2):
            rows = pl.ds(part * (tokens // 2), tokens // 2)
            copies.append(
                pltpu.make_async_copy(
                    grad_hbm.at[rows, pl.ds(side * half, half)],
                    target.at[rows, :],
                    sems.at[2 + 2 * side + part],
                )
            )
    for copy in copies:
        copy.start()
    copies[0].wait()
    copies[1].wait()
    gates = gates_ref[...]
    high = gates.astype(BF16).astype(F32)
    middle = (gates - high).astype(BF16).astype(F32)
    low = gates - high - middle
    notes = jnp.concatenate(
        [ids_ref[...].astype(F32), high, middle, low, jnp.zeros((8, tokens), F32)], axis=0
    ).astype(BF16)
    for target in (left_ref, right_ref):
        target[tokens : tokens + 16, :] = jnp.zeros((16, half), BF16)
        target[tokens : tokens + 16, 0:tokens] = notes
    slots, first = slots_from(ids_ref[...])
    table = jnp.where(first, gates[0:1, :], gates[1:2, :])
    slots_ref[...], table_ref[...] = slots, table
    for copy in copies[2:]:
        copy.wait()
    relay(right_ref, slots, table, 1, left_ref, slice(tokens + 16, None))
    relay(left_ref, slots, table, 2, right_ref, slice(tokens + 16, None))


def notes_of(ref, tokens):
    notes = ref[tokens : tokens + 16, 0:tokens].astype(F32)
    slots, first = slots_from(notes[0:2].astype(jnp.int32))
    gates = notes[2:4] + notes[4:6] + notes[6:8]
    return slots, jnp.where(first, gates[0:1, :], gates[1:2, :])


def relay(ref, slots, gates, k, out_ref, place, shift=0):
    tokens = slots.shape[1]
    rows_at = range(*place.indices(out_ref.shape[0]))
    mask = one_hot(slots, k, len(rows_at))
    pick = as_bf16(mask)
    if gates is not None:
        gate = jnp.sum(jnp.where(mask, gates[k : k + 1, :], 0.0), axis=1, keepdims=True)
    for at in range(0, ref.shape[1], GROUP):
        rows = jnp.dot(pick, ref[0:tokens, at : at + GROUP], preferred_element_type=F32)
        if gates is not None:
            rows = rows * gate
        out_ref[place, shift + at : shift + at + GROUP] = rows.astype(BF16)


def gather_near(own, by_x, by_y, blocks, direct, near_ref):
    (own_slots, own_gates), (x_slots, x_gates), (y_slots, y_gates) = own, by_x, by_y
    left_ref, right_ref, x_ref, y_ref = blocks
    capacity, half = near_ref.shape[0] // 3, left_ref.shape[1]
    here, at_x, at_y = (slice(k * capacity, (k + 1) * capacity) for k in range(3))
    relay(left_ref, own_slots, own_gates, 0, near_ref, here)
    relay(right_ref, own_slots, own_gates, 0, near_ref, here, half)
    relay(x_ref, x_slots, x_gates, 0, near_ref, at_x)
    near_ref[at_x, half:] = x_ref[direct, :]
    near_ref[at_y, 0:half] = y_ref[direct, :]
    relay(y_ref, y_slots, y_gates, 0, near_ref, at_y, half)


def relay_grads(left_ref, right_ref, x_ref, y_ref, slots_ref, table_ref, *refs):
    pass_left, pass_right, near_ref, others_ref = refs
    tokens = slots_ref.shape[1]
    x_notes, y_notes = notes_of(x_ref, tokens), notes_of(y_ref, tokens)
    others_ref[0:8, :], others_ref[8:16, :] = x_notes[0], y_notes[0]
    relay(x_ref, *x_notes, 2, pass_left, slice(None))
    relay(y_ref, *y_notes, 1, pass_right, slice(None))
    blocks = (left_ref, right_ref, x_ref, y_ref)
    own = (slots_ref[...], table_ref[...])
    gather_near(own, x_notes, y_notes, blocks, slice(tokens + 16, None), near_ref)


def relay_rows(left_ref, right_ref, x_ref, y_ref, slots_ref, others_ref, *refs):
    pass_left, pass_right, near_ref = refs
    by_x, by_y = (others_ref[0:8, :], None), (others_ref[8:16, :], None)
    relay(x_ref, *by_x, 2, pass_left, slice(None))
    relay(y_ref, *by_y, 1, pass_right, slice(None))
    blocks = (left_ref, right_ref, x_ref, y_ref)
    direct = slice(slots_ref.shape[1], None)
    gather_near((slots_ref[...], None), by_x, by_y, blocks, direct, near_ref)


def activate(value):
    square = value * value
    curve = jnp.tanh(GELU_C * (value + GELU_A * square * value))
    hidden = (0.5 * value * (1.0 + curve)).astype(BF16)
    slope = 0.5 * (1.0 + curve) + 0.5 * value * (1.0 - curve * curve) * (
        GELU_C * (1.0 + 3.0 * GELU_A * square)
    )
    return hidden, slope


def narrow(left_ref, right_ref, matrix_ref):
    half = left_ref.shape[1]
    return sum(
        lax.dot_general(
            ref[...], matrix_ref[:, at : at + half], (((1,), (1,)), ((), ())), preferred_element_type=F32
        )
        for ref, at in ((left_ref, 0), (right_ref, half))
    )


def back_products(near_ref, left_ref, right_ref, out_ref, near_back_ref, far_back_ref):
    near_back_ref[...] = hidden_grad(near_ref, out_ref)
    far_back_ref[...] = narrow(left_ref, right_ref, out_ref)


def experts_near(near_ref, back_ref, in_ref, out_ref, *refs):
    result_refs, grad_ref = refs[0:3], refs[3]
    hidden, slope = activate(hidden_grad(near_ref, in_ref))
    grad_ref[...] = (back_ref[...] * slope).astype(BF16)
    size = result_refs[0].shape[0]
    for at in range(0, out_ref.shape[1], CHUNK):
        cols = slice(at, at + CHUNK)
        rows = jnp.dot(hidden, out_ref[:, cols], preferred_element_type=F32).astype(BF16)
        for k in range(3):
            result_refs[k][:, cols] = rows[k * size : (k + 1) * size]


def weight_grads_near(near_ref, grad_ref, total_ref):
    total_ref[...] = lax.dot_general(
        near_ref[...], grad_ref[...], (((0,), (0,)), ((), ())), preferred_element_type=F32
    )


def finish_far(shards, *refs):
    left_ref, right_ref, back_ref, in_ref, total_ref = refs[0:5]
    hidden_ref, keep_ref, send_ref = refs[5:]

    hidden, slope = activate(narrow(left_ref, right_ref, in_ref))
    hidden_ref[...] = hidden
    grads = (back_ref[...] * slope).astype(BF16)
    halves = [
        lax.dot_general(ref[...], grads, (((0,), (0,)), ((), ())), preferred_element_type=F32)
        for ref in (left_ref, right_ref)
    ]
    block = total_ref.shape[0] // (2 * shards)
    core = lax.axis_index("seq")
    for shard in range(shards):
        full = halves[2 * shard // shards]
        at, there = (2 * shard) % shards * block, 2 * shard * block
        even = pack(full[at : at + block] + total_ref[there : there + block, :])
        odd = pack(
            full[at + block : at + 2 * block] + total_ref[there + block : there + 2 * block, :]
        )
        keep_ref[shard] = jnp.where(core == 0, even, odd)
        send_ref[shard] = jnp.where(core == 0, odd, even).astype(BF16)


def widen(hidden_ref, out_ref, result_ref):
    for at in range(0, out_ref.shape[1], CHUNK):
        cols = slice(at, at + CHUNK)
        result_ref[:, cols] = jnp.dot(
            hidden_ref[...], out_ref[:, cols], preferred_element_type=F32
        ).astype(BF16)


def dispatch_rows(count, slots_ref, left_ref, right_ref, *out_refs):
    half = left_ref.shape[1]
    slots = slots_ref[...]
    for k in range(count):
        pick = as_bf16(one_hot(slots, k, out_refs[k].shape[0]))
        for at in range(0, half, GROUP):
            cols = slice(at, at + GROUP)
            there = slice(half + at, half + at + GROUP)
            out_refs[k][:, cols] = jnp.dot(
                pick, left_ref[:, cols], preferred_element_type=F32
            ).astype(BF16)
            out_refs[k][:, there] = jnp.dot(
                pick, right_ref[:, cols], preferred_element_type=F32
            ).astype(BF16)


def forward(rows_ref, in_ref, out_ref, result_ref):
    hidden, slope = activate(
        lax.dot_general(
            rows_ref[...], in_ref[...], (((1,), (1,)), ((), ())), preferred_element_type=F32
        )
    )
    for at in range(0, out_ref.shape[1], CHUNK):
        cols = slice(at, at + CHUNK)
        result_ref[:, cols] = jnp.dot(
            hidden, out_ref[:, cols], preferred_element_type=F32
        ).astype(BF16)
    return slope


def hidden_grad(grad_ref, out_ref):
    return lax.dot_general(
        grad_ref[...], out_ref[...], (((1,), (1,)), ((), ())), preferred_element_type=F32
    )


def expert_first(count, *refs):
    rows_refs, grad_refs = refs[0:count], refs[count : 2 * count + 1]
    in_ref, out_ref = refs[2 * count + 1 : 2 * count + 3]
    result_refs = refs[2 * count + 3 : 3 * count + 3]
    back_refs, last_ref = refs[3 * count + 3 : 4 * count + 3], refs[4 * count + 3]
    for k in range(count):
        slope = forward(rows_refs[k], in_ref, out_ref, result_refs[k])
        back_refs[k][...] = (hidden_grad(grad_refs[k], out_ref) * slope).astype(BF16)
    last_ref[...] = hidden_grad(grad_refs[count], out_ref)


def expert_last(rows_ref, back_ref, in_ref, out_ref, result_ref, grad_ref):
    slope = forward(rows_ref, in_ref, out_ref, result_ref)
    grad_ref[...] = (back_ref[...] * slope).astype(BF16)


def sum_of_products(rows_refs, grad_refs):
    rows = jnp.concatenate([ref[...] for ref in rows_refs], axis=0)
    grads = jnp.concatenate([ref[...] for ref in grad_refs], axis=0)
    return lax.dot_general(rows, grads, (((0,), (0,)), ((), ())), preferred_element_type=F32)


def pack(block):
    rows, columns = block.shape
    full = columns // 128 * 128
    pieces = [block[:, at : at + 128] for at in range(0, full, 128)]
    pieces.append(
        jnp.concatenate([block[: rows // 2, full:], block[rows // 2 :, full:]], axis=1)
    )
    return jnp.concatenate(pieces, axis=0)


def unpack(packed, rows, columns):
    full = columns // 128 * 128
    last = packed[full // 128 * rows :, :]
    half = columns - full
    pieces = [packed[at * rows : (at + 1) * rows, :] for at in range(full // 128)]
    pieces.append(jnp.concatenate([last[:, :half], last[:, half:]], axis=0))
    return jnp.concatenate(pieces, axis=1)


def weight_grads_whole(count, *refs):
    refs[2 * count][...] = sum_of_products(refs[0:count], refs[count : 2 * count])


def add_cores(shards, keep_ref, other_ref, own_ref, *send_refs):
    me = lax.axis_index("dp")
    own_ref[...] = keep_ref[me] + other_ref[me].astype(F32)
    for k in range(1, shards):
        send_refs[k - 1][...] = (keep_ref[me ^ k] + other_ref[me ^ k].astype(F32)).astype(BF16)


def add_replicas(own_ref, *refs):
    total = own_ref[...]
    for ref in refs[:-1]:
        total = total + ref[...].astype(F32)
    _, rows, columns = refs[-1].shape
    refs[-1][0] = unpack(total, rows, columns)


def combine_here(slots_ref, gates_ref, stream_ref, here_ref, total_ref):
    mix_into(slots_ref, gates_ref, 0, stream_ref, (here_ref,), total_ref)


def combine_rest(slots_ref, gates_ref, base_ref, *refs):
    mix_into(slots_ref, gates_ref, 1, base_ref, refs[:-1], refs[-1])


def mix_into(slots_ref, gates_ref, first, base_ref, result_refs, out_ref):
    slots = slots_ref[...]
    gates = gates_ref[...].T
    picks = [
        as_bf16(one_hot(slots, first + k, ref.shape[0])) for k, ref in enumerate(result_refs)
    ]
    for at in range(0, base_ref.shape[1], CHUNK):
        cols = slice(at, at + CHUNK)
        total = base_ref[:, cols]
        for k, ref in enumerate(result_refs):
            row = lax.dot_general(
                picks[k], ref[:, cols], (((0,), (0,)), ((), ())), preferred_element_type=F32
            )
            total = total + row * gates[:, first + k : first + k + 1]
        out_ref[:, cols] = total.astype(out_ref.dtype)


def swap(value, axis, k):
    return lax.ppermute(value, axis, [(i, i ^ k) for i in range(lax.axis_size(axis))])


def per_device(
    queries, memory, residual, norm_gain, expert_ids, route_gates, weight_in, weight_out, layer_grad
):
    tokens, width = queries.shape
    hidden_width = weight_in.shape[2]
    experts, replicas, cores = (lax.axis_size(axis) for axis in ("expert", "dp", "seq"))
    capacity = (5 * tokens + 2 * experts - 1) // (2 * experts)
    capacity = (capacity + 15) // 16 * 16
    half = width // 2
    in_hbm = functools.partial(pltpu.with_memory_space_constraint, memory_space=pltpu.HBM)
    ids, gates = in_hbm(expert_ids.T), in_hbm(route_gates.T)
    layer_grad, queries, residual = in_hbm(layer_grad), in_hbm(queries), in_hbm(residual)
    matrix_in, matrix_out = weight_in[0].T, weight_out[0]
    table = shape((8, tokens), F32)
    vmem, hbm = pltpu.VMEM, pltpu.HBM

    if cores == 2:
        memories = [swap(memory, "seq", 1)]
        own_memory = in_hbm(memory)
    else:
        memories = []
        own_memory = in_hbm(lax.all_gather(memory, "seq", axis=1, tiled=True))
    parts = 1 + len(memories)
    dma = pltpu.SemaphoreType.DMA
    block = width // (replicas * cores)
    hops = experts == 4 and cores == 2 and replicas == 4 and block % 32 == 0
    hops = hops and hidden_width % 128 == 64
    extra = capacity if hops else 0
    attend_call = call(
        functools.partial(attend, parts, hops),
        [shape((tokens, width), F32)] + [shape((tokens + extra, half), BF16)] * 2,
        [vmem((tokens, width), BF16)] * 2
        + [vmem((width,), F32), vmem(own_memory.shape, BF16)]
        + [dma((width // CHUNK,))] * 2
        + [dma, dma],
        [vmem] + [hbm] * 4 + [vmem] * len(memories),
    )
    attend_inputs = (queries, residual, in_hbm(norm_gain), own_memory, *memories)
    integers = shape((8, tokens), jnp.int32)

    if hops:
        first_hop = shape((tokens + 16 + capacity, half), BF16)
        second_hop = shape((capacity, half), BF16)
        near = shape((3 * capacity, width), BF16)
        near_narrow = (3 * capacity, hidden_width)
        left, right, slots, gates = call(
            split_grads,
            [first_hop] * 2 + [integers, table],
            [vmem((2, tokens), jnp.int32), vmem((2, tokens), F32), dma((6,))],
            [hbm] * 3,
        )(ids, gates, layer_grad)
        by_x, by_y = swap(left, "expert", 1), swap(right, "expert", 2)
        stream, left_rows, right_rows = attend_call(slots, *attend_inputs)
        rows_x, rows_y = swap(left_rows, "expert", 1), swap(right_rows, "expert", 2)
        pass_left, pass_right, near_grads, others = call(
            relay_grads, [second_hop] * 2 + [near, shape((16, tokens), jnp.int32)]
        )(left, right, by_x, by_y, slots, gates)
        far_grads = (swap(pass_left, "expert", 2), swap(pass_right, "expert", 1))
        pass_left, pass_right, near_rows = call(relay_rows, [second_hop] * 2 + [near])(
            left_rows, right_rows, rows_x, rows_y, slots, others
        )
        far_rows = (swap(pass_left, "expert", 2), swap(pass_right, "expert", 1))
        back, far_back = call(
            back_products, [shape(near_narrow, F32), shape((capacity, hidden_width), F32)]
        )(near_grads, *far_grads, matrix_out)
        result_shape = shape((capacity, width), BF16)
        *results, near_pre = call(experts_near, [result_shape] * 3 + [shape(near_narrow, BF16)])(
            near_rows, back, matrix_in, matrix_out
        )
        total = call(weight_grads_near, shape((width, hidden_width), F32))(near_rows, near_pre)
        packed = (replicas, block * hidden_width // 128, 128)
        hidden, keep, send = call(
            functools.partial(finish_far, replicas),
            [shape((capacity, hidden_width), BF16), shape(packed, F32), shape(packed, BF16)],
        )(*far_rows, far_back, matrix_in, total)
        results.append(call(widen, result_shape)(hidden, matrix_out))
        own, *sends = call(
            functools.partial(add_cores, replicas),
            [shape(packed[1:], F32)] + [shape(packed[1:], BF16)] * (replicas - 1),
        )(keep, swap(send, "seq", 1))
        received = [swap(sends[k - 1], "dp", k) for k in (2, 1, 3)]
        grads_here = call(add_replicas, shape((1, block, hidden_width), F32))(own, *received)
    else:
        rows_shape = [shape((capacity, width), BF16)] * experts
        *grads, slots, gates = call(
            functools.partial(dispatch_grads, experts),
            rows_shape + [integers, table],
            [vmem((tokens, width), BF16), dma((width // CHUNK,))],
            [vmem, vmem, hbm],
        )(expert_ids.T, route_gates.T, layer_grad)
        grads = [grads[0]] + [swap(grads[k], "expert", k) for k in range(1, experts)]
        stream, left, right = attend_call(slots, *attend_inputs)
        rows = call(functools.partial(dispatch_rows, experts), rows_shape)(slots, left, right)
        rows = [rows[0]] + [swap(rows[k], "expert", k) for k in range(1, experts)]
        last = experts - 1
        back_shape = shape((capacity, hidden_width), BF16)
        outs = call(
            functools.partial(expert_first, last),
            rows_shape[:last] + [back_shape] * last + [shape((capacity, hidden_width), F32)],
        )(*rows[:last], *grads, matrix_in, matrix_out)
        result, back = call(expert_last, [rows_shape[0], back_shape])(
            rows[last], outs[2 * last], matrix_in, matrix_out
        )
        results = list(outs[:last]) + [result]
        whole = call(
            functools.partial(weight_grads_whole, experts), shape((width, hidden_width), F32)
        )(*rows, *outs[last : 2 * last], back)
        grads_here = lax.psum_scatter(whole, ("dp", "seq"), scatter_dimension=0, tiled=True)[None]
    results = [results[0]] + [swap(results[k], "expert", k) for k in range(1, experts)]

    base = call(combine_here, shape((tokens, width), F32))(slots, gates, stream, results[0])
    layer_output = call(combine_rest, shape((tokens, width), BF16))(
        slots, gates, base, *results[1:]
    )
    return layer_output, grads_here


def solution(mesh):
    rows = P(("dp", "expert", "seq"), None)
    return jax.shard_map(
        per_device,
        mesh=mesh,
        in_specs=(
            rows,
            P(None, ("dp", "expert", "seq"), None),
            rows,
            P(),
            rows,
            rows,
            P("expert", None, None),
            P("expert", None, None),
            rows,
        ),
        out_specs=(rows, P("expert", ("dp", "seq"), None)),
        check_vma=False,
    )
```
